128 devices in a mesh: mesh: 16 (over y, x), span: 8 (over z, core).
Axes of the slice: x: 4, y: 4, z: 4, core: 2. Of those that a mesh axis runs over, the one named last changes fastest.
Arguments:
- velocity_q: float32 [512, 49, 2048], P('span', None, 'mesh'), may hold values from -6 to 6
- advecting: bfloat16 [2, 512, 49, 2048], P(None, 'span', None, 'mesh'), may hold values from -0.01171875 to 0.01171875
- damping: float32 [49, 2048], P(None, 'mesh'), may hold values from 0.02 to 8
Outputs:
- q_new: float32 [512, 49, 2048], P('span', None, 'mesh')
The draws below stay inside these ranges and needn't reach their ends.
All inputs are finite; a program needn't handle non-finite values.
Results may differ from the reference program's by a relative error of at most 0.0003.
Values sent between devices are 32-bit elements; how exact they have to be, the bound alone decides.
No kernel may reach another device: no remote copies, remote signals or barrier semaphores. Data moves between devices by JAX's collectives and lax.ppermute only.
A program may use at most 128 MiB of HBM per device.

```python
import math
import jax
import jax.numpy as jnp
import numpy as np
from jax import lax

ORDER = 6
NODES = 49
EY = 128
PL_DEV = 64
ITERS = 8
PLANES = 512
WAVES = 168
KEPT = 336
ELEMS = 2048
N_SPAN = 8


def block_scale(own_key, extent, cuts, least, largest):
    gain = 1.0
    for position, blocks in cuts:
        steps = jax.random.uniform(jax.random.fold_in(jax.random.fold_in(own_key, 6), position), (blocks,), jnp.float32, least / len(cuts), largest / len(cuts))
        gain = gain * jnp.repeat(jnp.exp(steps), extent[position] // blocks).reshape((-1,) + (1,) * (len(extent) - 1 - position))
    return gain


def bell_draw(stream_key, shape, deviation, reach, split=(), kind=jnp.bfloat16):
    values = jax.random.normal(stream_key, shape, jnp.float32) * deviation
    if len(split) > 0:
        values = block_scale(stream_key, shape, split, -0.22, 0.18) * values
    return jnp.clip(values, min=-reach, max=reach).astype(kind)


def setup_inputs(seed: int = 0) -> dict:
    key_of = jax.random.split(jax.random.key(seed), 4)
    velocity_q = bell_draw(key_of[0], (PLANES, NODES, ELEMS), 1.0, 6.0, ((0, 8), (2, 16)), jnp.float32)
    advecting = bell_draw(key_of[1], (2, PLANES, NODES, ELEMS), 0.002, 0.01171875, ((1, 8), (3, 16)))
    damping = jnp.clip(jnp.exp(math.log(8.0) - 5.9914646 * jax.random.uniform(key_of[2], (NODES, ELEMS), jnp.float32) ** block_scale(key_of[2], (NODES, ELEMS), ((1, 16),), -0.2, 0.2)), 0.02, 8.0)
    return {"velocity_q": velocity_q, "advecting": advecting, "damping": damping}


LAMBDA0 = 0.1
VISCOSITY = 0.02
PENALTY = 100.0
BETA = 0.02
HIGH = lax.Precision.HIGHEST


def gll_tables(degree):
    side_nodes = degree + 1
    points = [-math.cos(math.pi * node_index / degree) for node_index in range(side_nodes)]
    values = [1.0] * side_nodes
    for sweep_index in range(60):
        updated = []
        new_values = []
        for node_point in points:
            lower_poly = 1.0
            legendre_now = node_point
            for order_step in range(2, degree + 1):
                next_poly = ((2 * order_step - 1) * node_point * legendre_now - (order_step - 1) * lower_poly) / order_step
                lower_poly = legendre_now
                legendre_now = next_poly
            updated.append(node_point - (node_point * legendre_now - lower_poly) / (side_nodes * legendre_now))
            new_values.append(legendre_now)
        points = updated
        values = new_values
    weights = [2.0 / (degree * side_nodes * entry_value * entry_value) for entry_value in values]
    derivative = np.zeros((side_nodes, side_nodes))
    for row_index in range(side_nodes):
        for col_index in range(side_nodes):
            if row_index != col_index:
                derivative[row_index, col_index] = values[row_index] / (values[col_index] * (points[row_index] - points[col_index]))
    derivative[0, 0] = -degree * side_nodes / 4.0
    derivative[degree, degree] = degree * side_nodes / 4.0
    return jnp.asarray(np.array(weights), jnp.float32), jnp.asarray(derivative, jnp.float32)


def fourier_table(number, planes, wave_count):
    coeff_index = jnp.arange(number, dtype=jnp.int32)[:, None]
    plane_index = jnp.arange(planes, dtype=jnp.int32)[None, :]
    cosine = coeff_index < wave_count
    wavenumber = jnp.where(cosine, coeff_index, coeff_index - wave_count + 1)
    phases = ((wavenumber * plane_index) % planes).astype(jnp.float32) * (2.0 * math.pi / planes)
    return jnp.where(cosine, jnp.cos(phases), jnp.sin(phases)), wavenumber[:, 0]


def along_first(derivative, values):
    return jnp.einsum('ia,majxy->mijxy', derivative, values, precision=HIGH)


def along_second(derivative, values):
    return jnp.einsum('jb,mibxy->mijxy', derivative, values, precision=HIGH)


def shift_later(values):
    return jnp.pad(values, ((0, 0), (0, 0), (1, 0), (0, 0)))[:, :, :-1]


def shift_earlier(values):
    return jnp.pad(values, ((0, 0), (0, 0), (0, 1), (0, 0)))[:, :, 1:]


def face_terms(first_value, last_value, first_slope, last_slope, before_value, before_slope, after_value, after_slope, weights, derivative, degree):
    face_weight = weights[None, :, None, None]
    jump_after = last_value - after_value
    jump_before = before_value - first_value
    coef_after = face_weight * (PENALTY * jump_after - 0.5 * (last_slope + after_slope))
    coef_before = face_weight * (PENALTY * jump_before - 0.5 * (before_slope + first_slope))
    spread = -0.5 * (jnp.einsum('a,mjxy->majxy', derivative[degree], face_weight * jump_after, precision=HIGH) + jnp.einsum('a,mjxy->majxy', derivative[0], face_weight * jump_before, precision=HIGH))
    spread = spread.at[:, degree].add(coef_after)
    spread = spread.at[:, 0].add(-coef_before)
    return spread


def helmholtz(mode_field, shifts, damping, weights, derivative, degree):
    mass_weights = (weights[:, None] * weights[None, :])[:, :, None, None]
    grad_x = along_first(derivative, mode_field)
    grad_y = along_second(derivative, mode_field)
    result = jnp.einsum('ai,majxy->mijxy', derivative, mass_weights * grad_x, precision=HIGH)
    result = result + jnp.einsum('bj,mibxy->mijxy', derivative, mass_weights * grad_y, precision=HIGH)
    result = result + (shifts[:, None, None, None, None] + damping) * mass_weights * mode_field
    low_value = mode_field[:, :, 0]
    high_value = mode_field[:, :, degree]
    low_slope = grad_y[:, :, 0]
    high_slope = grad_y[:, :, degree]
    y_terms = face_terms(low_value, high_value, low_slope, high_slope, jnp.roll(high_value, 1, axis=3), jnp.roll(high_slope, 1, axis=3), jnp.roll(low_value, -1, axis=3), jnp.roll(low_slope, -1, axis=3), weights, derivative, degree)
    result = result + jnp.swapaxes(y_terms, 1, 2)
    first_value = mode_field[:, 0]
    last_value = mode_field[:, degree]
    first_slope = grad_x[:, 0]
    last_slope = grad_x[:, degree]
    x_terms = face_terms(first_value, last_value, first_slope, last_slope, shift_later(last_value), shift_later(last_slope), shift_earlier(first_value), shift_earlier(first_slope), weights, derivative, degree)
    return result + x_terms


def forcing_term(block_q, block_velocity, weights, derivative, degree, columns_x):
    side_nodes = degree + 1
    planes = block_q.shape[0]
    local_q = block_q.reshape(planes, side_nodes, side_nodes, columns_x, EY)
    velocity = block_velocity.astype(jnp.float32).reshape(2, planes, side_nodes, side_nodes, columns_x, EY)
    edge_weight = weights[0]
    grad_x = along_first(derivative, local_q)
    grad_y = along_second(derivative, local_q)
    first_face = local_q[:, 0]
    last_face = local_q[:, degree]
    grad_x = grad_x.at[:, degree].add((shift_earlier(first_face) - last_face) / (2.0 * edge_weight))
    grad_x = grad_x.at[:, 0].add(-(shift_later(last_face) - first_face) / (2.0 * edge_weight))
    low_side = local_q[:, :, 0]
    high_side = local_q[:, :, degree]
    grad_y = grad_y.at[:, :, degree].add((jnp.roll(low_side, -1, axis=3) - high_side) / (2.0 * edge_weight))
    grad_y = grad_y.at[:, :, 0].add(-(jnp.roll(high_side, 1, axis=3) - low_side) / (2.0 * edge_weight))
    forcing = LAMBDA0 * local_q - (velocity[0] * grad_x + velocity[1] * grad_y) / VISCOSITY
    return forcing.reshape(planes, -1)


def reference(velocity_q, advecting, damping):
    degree = ORDER
    side_nodes = degree + 1
    columns_x = ELEMS // EY
    weights, derivative = gll_tables(degree)
    basis_table, wavenumber = fourier_table(KEPT, PLANES, WAVES)
    coeff_index = jnp.arange(KEPT, dtype=jnp.int32)
    scaling = jnp.where(coeff_index == 0, 1.0 / PLANES, 2.0 / PLANES).astype(jnp.float32)
    forward = basis_table * scaling[:, None]

    def add_block(running, block_index):
        first_plane = (block_index * PL_DEV).astype(jnp.int32)
        block_q = lax.dynamic_slice_in_dim(velocity_q, first_plane, PL_DEV, 0)
        block_velocity = lax.dynamic_slice_in_dim(advecting, first_plane, PL_DEV, 1)
        forcing = forcing_term(block_q, block_velocity, weights, derivative, degree, columns_x)
        block_table = lax.dynamic_slice_in_dim(forward, first_plane, PL_DEV, 1)
        return running + jnp.dot(block_table, forcing, precision=HIGH, preferred_element_type=jnp.float32), None

    spectra = lax.scan(add_block, jnp.zeros((KEPT, NODES * ELEMS), jnp.float32), jnp.arange(N_SPAN, dtype=jnp.int32))[0]
    mass_weights = (weights[:, None] * weights[None, :])[:, :, None, None]
    right_side = mass_weights * spectra.reshape(KEPT, side_nodes, side_nodes, columns_x, EY)
    shifts = LAMBDA0 + (BETA * wavenumber.astype(jnp.float32)) ** 2
    damp_nodes = damping.reshape(side_nodes, side_nodes, columns_x, EY)

    def solve_block(pieces):
        block_rhs, block_shifts = pieces
        solution = jnp.zeros_like(block_rhs)
        residual = block_rhs
        direction = block_rhs
        res_norm = jnp.sum(residual * residual, axis=(1, 2, 3, 4))
        for iteration in range(ITERS):
            operated = helmholtz(direction, block_shifts, damp_nodes, weights, derivative, degree)
            step_size = res_norm / jnp.sum(direction * operated, axis=(1, 2, 3, 4))
            solution = solution + step_size[:, None, None, None, None] * direction
            residual = residual - step_size[:, None, None, None, None] * operated
            new_norm = jnp.sum(residual * residual, axis=(1, 2, 3, 4))
            direction = residual + (new_norm / res_norm)[:, None, None, None, None] * direction
            res_norm = new_norm
        return solution

    block_count = KEPT // N_SPAN
    solved = lax.map(solve_block, (right_side.reshape(N_SPAN, block_count, side_nodes, side_nodes, columns_x, EY), shifts.reshape(N_SPAN, block_count)))
    mode_values = solved.reshape(KEPT, -1)
    result = jnp.dot(basis_table.T, mode_values, precision=HIGH, preferred_element_type=jnp.float32)
    return result.reshape(PLANES, NODES, ELEMS)
```

```python
import math

import jax
import jax.numpy as jnp
import ml_dtypes
import numpy as np
from jax import lax
from jax.experimental import pallas as pl
from jax.experimental.pallas import tpu as pltpu
from jax.sharding import PartitionSpec as P

ORDER = 6
SIDE = 7
NODES = 49
EY = 128
COLS = 16
PLANES = 512
PL_DEV = 64
N_SPAN = 8
N_DEV = 128
WAVES = 168
KEPT = 336
M_DEV = 3
M_ALL = N_DEV * M_DEV
SHARE = 8 * EY
ITERS = 8

LAMBDA0 = 0.1
VISCOSITY = 0.02
PENALTY = 100.0
BETA = 0.02
VMEM = 56 * 1024 * 1024


def gll_tables(degree):
    side_nodes = degree + 1
    points = [-math.cos(math.pi * n / degree) for n in range(side_nodes)]
    values = [1.0] * side_nodes
    for _ in range(60):
        updated = []
        new_values = []
        for point in points:
            lower = 1.0
            now = point
            for step in range(2, degree + 1):
                lower, now = now, ((2 * step - 1) * point * now - (step - 1) * lower) / step
            updated.append(point - (point * now - lower) / (side_nodes * now))
            new_values.append(now)
        points = updated
        values = new_values
    weights = np.array([2.0 / (degree * side_nodes * v * v) for v in values])
    derivative = np.zeros((side_nodes, side_nodes))
    for row in range(side_nodes):
        for col in range(side_nodes):
            if row != col:
                derivative[row, col] = values[row] / (values[col] * (points[row] - points[col]))
    derivative[0, 0] = -degree * side_nodes / 4.0
    derivative[degree, degree] = degree * side_nodes / 4.0
    return weights, derivative


W, D = gll_tables(ORDER)


def fourier_table():
    c = np.arange(M_ALL)[:, None]
    p = np.arange(PLANES)[None, :]
    k = np.where(c < WAVES, c, c - WAVES + 1)
    phases = ((k * p) % PLANES) * (2.0 * math.pi / PLANES)
    table = np.where(c < WAVES, np.cos(phases), np.sin(phases))
    return np.where(c < KEPT, table, 0.0)


def in_two(table):
    table = table.astype(np.float32)
    high = table.astype(ml_dtypes.bfloat16)
    low = (table - high.astype(np.float32)).astype(ml_dtypes.bfloat16)
    return jnp.asarray(high), jnp.asarray(low)


def split(x):
    high = x.astype(jnp.bfloat16)
    low = (x - high.astype(jnp.float32)).astype(jnp.bfloat16)
    return high, low


def dot(a, b):
    return jnp.dot(a, b, preferred_element_type=jnp.float32)


def combine(coefs, values):
    total = None
    for c, v in zip(coefs, values):
        if c == 0.0:
            continue
        term = v * np.float32(c)
        total = term if total is None else total + term
    return total


def forcing_kernel(q_ref, left_ref, right_ref, a_ref, out_ref):
    table = D / VISCOSITY
    edge = 1.0 / (2.0 * W[0] * VISCOSITY)
    own = table.copy()
    own[6, 6] -= edge
    own[0, 0] += edge
    edge = np.float32(edge)

    def block(b, carry):
        rows = pl.ds(pl.multiple_of(b * 16, 16), 16)
        for i in range(SIDE):
            line = [q_ref[i * SIDE + j, rows, :] for j in range(SIDE)]
            gy = [combine(own[j], line) for j in range(SIDE)]
            gy[6] = gy[6] + edge * pltpu.roll(line[0], EY - 1, 1)
            gy[0] = gy[0] - edge * pltpu.roll(line[6], 1, 1)
            for j in range(SIDE):
                gx = combine(own[i], [q_ref[a * SIDE + j, rows, :] for a in range(SIDE)])
                if i == 6:
                    gx = gx + edge * right_ref[j, rows, :]
                if i == 0:
                    gx = gx - edge * left_ref[j, rows, :]
                n = i * SIDE + j
                ax = a_ref[0, n, rows, :].astype(jnp.float32)
                ay = a_ref[1, n, rows, :].astype(jnp.float32)
                out_ref[i, rows, j * EY : (j + 1) * EY] = (
                    np.float32(LAMBDA0) * line[j] - (ax * gx + ay * gy[j])
                )
        return carry

    lax.fori_loop(0, PL_DEV // 16, block, 0)
    out_ref[7] = jnp.zeros((PL_DEV, SIDE * EY), jnp.float32)


def forward_kernel(x_ref, high_ref, low_ref, out_ref):
    for start, width in ((0, 2), (2, 2), (4, 2), (6, 1)):
        x = x_ref[:, start * EY : (start + width) * EY]
        xh, xl = split(x)
        res = dot(high_ref[...], xh) + (dot(high_ref[...], xl) + dot(low_ref[...], xh))
        for g in range(width):
            out_ref[pl.ds(start + g, M_ALL, stride=8), :] = res[:, g * EY : (g + 1) * EY]
    out_ref[pl.ds(7, M_ALL, stride=8), :] = jnp.zeros((M_ALL, EY), jnp.float32)


def inverse_kernel(x_ref, high_ref, low_ref, out_ref):
    for start, width in ((0, 2), (2, 2), (4, 2), (6, 1)):
        x = jnp.concatenate(
            [x_ref[pl.ds(start + g, M_ALL, stride=8), :] for g in range(width)], axis=1
        )
        xh, xl = split(x)
        res = dot(high_ref[...], xh) + (dot(high_ref[...], xl) + dot(low_ref[...], xh))
        out_ref[:, start * EY : (start + width) * EY] = res


def solve_tables():
    own = D.T @ np.diag(W) @ D
    own[6, 6] += PENALTY
    own[6, :] -= D[6, :] / 2
    own[:, 6] -= D[6, :] / 2
    own[0, 0] += PENALTY
    own[0, :] += D[0, :] / 2
    own[:, 0] += D[0, :] / 2
    return own


OWN = solve_tables()


def line_image(v, from_next, from_before):
    even = [v[0] + v[6], v[1] + v[5], v[2] + v[4], v[3]]
    odd = [v[0] - v[6], v[1] - v[5], v[2] - v[4]]
    d6 = D[6]
    d_even = [(d6[a] + d6[6 - a]) / 2 for a in range(3)] + [d6[3]]
    d_odd = [(d6[a] - d6[6 - a]) / 2 for a in range(3)]
    half_even = combine([c / 2 for c in d_even], even)
    half_odd = combine([c / 2 for c in d_odd], odd)
    penalty = np.float32(PENALTY)
    first = penalty * v[0] + (half_odd - half_even)
    last = penalty * v[6] - (half_even + half_odd)
    next_value = from_next(v[0])
    next_first = from_next(first)
    before_value = from_before(v[6])
    before_last = from_before(last)
    sum_value = next_value + before_value
    dif_value = next_value - before_value
    out = [None] * SIDE
    for i in range(3):
        e = combine(
            [(OWN[i, a] + OWN[i, 6 - a]) / 2 for a in range(3)] + [OWN[i, 3], d_even[i] / 2],
            even + [sum_value],
        )
        o = combine(
            [(OWN[i, a] - OWN[i, 6 - a]) / 2 for a in range(3)] + [d_odd[i] / 2],
            odd + [dif_value],
        )
        out[i] = e + o
        out[6 - i] = e - o
    out[3] = combine([OWN[3, a] for a in range(4)] + [d6[3] / 2], even + [sum_value])
    out[6] = out[6] - next_first
    out[0] = out[0] - before_last
    return out


def whole_sum(x):
    return jnp.sum(jnp.sum(x, axis=0, keepdims=True), axis=1, keepdims=True)


def solve_kernel(shift_ref, idle_ref, b_ref, damp_ref, out_ref, mass_ref, x_ref, r_ref, p_ref, q_ref):
    stride = N_SPAN * M_DEV * 8
    column = lax.broadcasted_iota(jnp.int32, (COLS, EY), 0)
    not_last = column < COLS - 1
    not_first = column > 0

    def x_next(v):
        return jnp.where(not_last, pltpu.roll(v, COLS - 1, 0), 0.0)

    def x_before(v):
        return jnp.where(not_first, pltpu.roll(v, 1, 0), 0.0)

    def y_next(v):
        return pltpu.roll(v, EY - 1, 1)

    def y_before(v):
        return pltpu.roll(v, 1, 1)

    zero = jnp.zeros((COLS, EY), jnp.float32)

    def one_mode(mode, carry):
        shift = shift_ref[mode]
        idle = idle_ref[mode]
        norm = zero
        for i in range(SIDE):
            for j in range(SIDE):
                n = i * SIDE + j
                w = np.float32(W[i] * W[j])
                rows = b_ref[pl.ds(i * M_DEV * 8 + mode * 8 + j, COLS, stride=stride), :]
                rhs = w * rows
                r_ref[n] = rhs
                p_ref[n] = zero
                x_ref[n] = zero
                mass_ref[n] = w * (damp_ref[n] + shift)
                norm = norm + rhs * rhs
        norm = whole_sum(norm)

        def iteration(step, state):
            norm, ratio = state
            for j in range(SIDE):
                line = []
                for i in range(SIDE):
                    n = i * SIDE + j
                    p = r_ref[n] + ratio * p_ref[n]
                    p_ref[n] = p
                    line.append(p)
                image = line_image(line, x_next, x_before)
                for i in range(SIDE):
                    n = i * SIDE + j
                    q_ref[n] = np.float32(W[j]) * image[i] + mass_ref[n] * line[i]
            curve = zero
            for i in range(SIDE):
                line = [p_ref[i * SIDE + j] for j in range(SIDE)]
                image = line_image(line, y_next, y_before)
                for j in range(SIDE):
                    n = i * SIDE + j
                    q = q_ref[n] + np.float32(W[i]) * image[j]
                    q_ref[n] = q
                    curve = curve + q * line[j]
            alpha = norm / (whole_sum(curve) + idle)
            fresh = zero
            for n in range(NODES):
                x_ref[n] = x_ref[n] + alpha * p_ref[n]
                r = r_ref[n] - alpha * q_ref[n]
                r_ref[n] = r
                fresh = fresh + r * r
            fresh = whole_sum(fresh)
            return fresh, fresh / (norm + idle)

        lax.fori_loop(0, ITERS, iteration, (norm, jnp.zeros((1, 1), jnp.float32)))
        for i in range(SIDE):
            for j in range(SIDE):
                out_ref[pl.ds(i * M_DEV * 8 + mode * 8 + j, COLS, stride=stride), :] = x_ref[i * SIDE + j]
        return carry

    lax.fori_loop(0, M_DEV, one_mode, 0)
    blank = jnp.zeros((COLS, EY), jnp.float32)
    for row in range(SIDE * M_DEV * 8, stride):
        out_ref[pl.ds(row, COLS, stride=stride), :] = blank
    for i in range(SIDE):
        for mode in range(M_DEV):
            out_ref[pl.ds(i * M_DEV * 8 + mode * 8 + 7, COLS, stride=stride), :] = blank


def call(kernel, shape, scratch=(), smem=0, n_in=0):
    full = pl.BlockSpec(memory_space=pltpu.VMEM)
    scalar = pl.BlockSpec(memory_space=pltpu.SMEM)
    return pl.pallas_call(
        kernel,
        out_shape=jax.ShapeDtypeStruct(shape, jnp.float32),
        in_specs=[scalar] * smem + [full] * n_in,
        out_specs=full,
        scratch_shapes=[pltpu.VMEM(s, jnp.float32) for s in scratch],
        compiler_params=pltpu.CompilerParams(vmem_limit_bytes=VMEM),
    )


def body(velocity_q, advecting, damping):
    everyone = ("mesh", "span")
    columns = lax.axis_size("mesh")
    up = [(i, i + 1) for i in range(columns - 1)]
    down = [(j, i) for i, j in up]
    q_nodes = jnp.transpose(velocity_q, (1, 0, 2))
    a_nodes = jnp.transpose(advecting, (0, 2, 1, 3))
    from_left = lax.ppermute(q_nodes[NODES - SIDE :], "mesh", up)
    from_right = lax.ppermute(q_nodes[:SIDE], "mesh", down)
    damp_nodes = lax.all_gather(damping, "mesh", axis=1, tiled=False)

    forcing = call(forcing_kernel, (N_SPAN, PL_DEV, SIDE * EY), n_in=4)(
        q_nodes, from_left, from_right, a_nodes
    )
    planes = lax.all_to_all(forcing, "span", split_axis=0, concat_axis=0, tiled=True)

    table = fourier_table()
    scale = np.where(np.arange(M_ALL) == 0, 1.0 / PLANES, 2.0 / PLANES)[:, None]
    spectra = call(forward_kernel, (M_ALL * 8, EY), n_in=3)(
        planes.reshape(PLANES, SIDE * EY), *in_two(table * scale)
    )
    mine = lax.all_to_all(
        spectra.reshape(N_DEV, M_DEV * 8, EY), everyone, split_axis=0, concat_axis=0, tiled=True
    )

    device = lax.axis_index("mesh") * N_SPAN + lax.axis_index("span")
    coef = device * M_DEV + jnp.arange(M_DEV, dtype=jnp.int32)
    wave = jnp.where(coef < WAVES, coef, coef - WAVES + 1).astype(jnp.float32)
    shifts = LAMBDA0 + (BETA * wave) ** 2
    idle = jnp.where(coef < KEPT, 0.0, 1.0).astype(jnp.float32)
    field = (NODES, COLS, EY)
    solved = call(
        solve_kernel, (N_DEV * M_DEV * 8, EY), scratch=(field,) * 5, smem=2, n_in=2
    )(shifts, idle, mine.reshape(N_DEV * M_DEV * 8, EY), damp_nodes)

    modes = lax.all_to_all(
        solved.reshape(N_DEV, M_DEV * 8, EY), everyone, split_axis=0, concat_axis=0, tiled=True
    )
    physical = call(inverse_kernel, (PLANES, SIDE * EY), n_in=3)(
        modes.reshape(M_ALL * 8, EY), *in_two(table.T)
    )
    back = lax.all_to_all(
        physical.reshape(N_SPAN, PL_DEV, SIDE * EY), "span", split_axis=0, concat_axis=0, tiled=True
    )
    back = back[:SIDE].reshape(SIDE, PL_DEV, SIDE, EY)
    return jnp.transpose(back, (1, 0, 2, 3)).reshape(PL_DEV, NODES, EY)


def solution(mesh):
    placed = (P("span", None, "mesh"), P(None, "span", None, "mesh"), P(None, "mesh"))
    return jax.shard_map(
        body, mesh=mesh, in_specs=placed, out_specs=P("span", None, "mesh"), check_vma=False
    )
```

```python
import math

import jax
import jax.numpy as jnp
import ml_dtypes
import numpy as np
from jax import lax
from jax.experimental import pallas as pl
from jax.experimental.pallas import tpu as pltpu
from jax.sharding import Mesh, PartitionSpec as P

ORDER = 6
SIDE = 7
NODES = 49
EY = 128
COLS = 16
PLANES = 512
PL_DEV = 64
N_SPAN = 8
N_DEV = 128
WAVES = 168
KEPT = 336
M_DEV = 3
M_ALL = N_DEV * M_DEV
GROUPS = 6
PIECE = 16
ROWS = GROUPS * PL_DEV + 8
PAIR = GROUPS * M_DEV + 1
PADDED = 56
ITERS = 8

LAMBDA0 = 0.1
VISCOSITY = 0.02
PENALTY = 100.0
BETA = 0.02
VMEM = 16 * 1024 * 1024


def gll_tables(degree):
    side_nodes = degree + 1
    points = [-math.cos(math.pi * n / degree) for n in range(side_nodes)]
    values = [1.0] * side_nodes
    for _ in range(60):
        updated = []
        new_values = []
        for point in points:
            lower = 1.0
            now = point
            for step in range(2, degree + 1):
                lower, now = now, ((2 * step - 1) * point * now - (step - 1) * lower) / step
            updated.append(point - (point * now - lower) / (side_nodes * now))
            new_values.append(now)
        points = updated
        values = new_values
    weights = np.array([2.0 / (degree * side_nodes * v * v) for v in values])
    derivative = np.zeros((side_nodes, side_nodes))
    for row in range(side_nodes):
        for col in range(side_nodes):
            if row != col:
                derivative[row, col] = values[row] / (values[col] * (points[row] - points[col]))
    derivative[0, 0] = -degree * side_nodes / 4.0
    derivative[degree, degree] = degree * side_nodes / 4.0
    return weights, derivative


W, D = gll_tables(ORDER)
EDGE = 1.0 / (2.0 * W[0] * VISCOSITY)


def fourier_table():
    row = np.arange(M_ALL)[:, None]
    c = row % N_DEV * M_DEV + row // N_DEV
    p = np.arange(PLANES)[None, :]
    k = np.where(c < WAVES, c, c - WAVES + 1)
    phases = ((k * p) % PLANES) * (2.0 * math.pi / PLANES)
    table = np.where(c < WAVES, np.cos(phases), np.sin(phases))
    scale = np.where(c == 0, 1.0 / PLANES, 2.0 / PLANES)
    table = np.where(c < KEPT, table, 0.0)
    return table * scale, table.T


def in_two(table):
    table = table.astype(np.float32)
    high = table.astype(ml_dtypes.bfloat16)
    low = (table - high.astype(np.float32)).astype(ml_dtypes.bfloat16)
    return jnp.asarray(high), jnp.asarray(low)


def split(x):
    high = x.astype(jnp.bfloat16)
    low = (x - high.astype(jnp.float32)).astype(jnp.bfloat16)
    return high, low


def dot(a, b):
    return jnp.dot(a, b, preferred_element_type=jnp.float32)


def combine(coefs, values):
    total = None
    for c, v in zip(coefs, values):
        if c == 0.0:
            continue
        term = v * np.float32(c)
        total = term if total is None else total + term
    return total


def turn(x, by):
    by = by % EY
    return pltpu.roll(x, by, 1) if by else x


def piece_of(shape):
    return lax.broadcasted_iota(jnp.int32, shape, 1) // PIECE


def pack(blocks, turns):
    piece = piece_of(blocks[0].shape)
    out = turn(blocks[0], turns[0])
    for h in range(1, len(blocks)):
        out = jnp.where(piece == h, turn(blocks[h], turns[h]), out)
    return out


def inner_kernel(q_ref, a_ref, out_ref):
    table = D / VISCOSITY
    own = table.copy()
    own[6, 6] -= EDGE
    own[0, 0] += EDGE
    edge = np.float32(EDGE)

    def block(b, carry):
        rows = pl.ds(pl.multiple_of(b * 16, 16), 16)
        for i in range(SIDE):
            line = [q_ref[i * SIDE + j, rows, :] for j in range(SIDE)]
            gy = [combine(own[j], line) for j in range(SIDE)]
            gy[6] = gy[6] + edge * pltpu.roll(line[0], EY - 1, 1)
            gy[0] = gy[0] - edge * pltpu.roll(line[6], 1, 1)
            for j in range(SIDE):
                n = i * SIDE + j
                gx = combine(own[i], [q_ref[a * SIDE + j, rows, :] for a in range(SIDE)])
                ax = a_ref[0, n, rows, :].astype(jnp.float32)
                ay = a_ref[1, n, rows, :].astype(jnp.float32)
                out_ref[n, rows, :] = np.float32(LAMBDA0) * line[j] - (ax * gx + ay * gy[j])
        return carry

    lax.fori_loop(0, PL_DEV // 16, block, 0)


def outer_kernel(
    place_ref, inner_ref, left_ref, right_ref, across_ref, damp_ref, a_ref, out_ref, row_ref, last_ref
):
    column = place_ref[0]
    has_left = jnp.where(column > 0, 1.0, 0.0)
    has_right = jnp.where(column < COLS - 1, 1.0, 0.0)
    edge = np.float32(EDGE)
    for n in range(NODES):
        target = last_ref if n == NODES - 1 else out_ref.at[n // GROUPS]
        start = 0 if n == NODES - 1 else n % GROUPS * PL_DEV
        j = n % SIDE
        face = slice(j * PL_DEV, (j + 1) * PL_DEV)
        value = inner_ref[n]
        if n < SIDE:
            value = value + (edge * has_left) * left_ref[face, :] * a_ref[0, n].astype(jnp.float32)
        if n >= NODES - SIDE:
            value = value - (edge * has_right) * right_ref[face, :] * a_ref[0, n].astype(jnp.float32)
        target[start : start + PL_DEV, :] = value
    for s in range(N_SPAN):
        blocks = [last_ref[8 * h : 8 * h + 8, :] for h in range(8)]
        out_ref[s, GROUPS * PL_DEV :, :] = pack(blocks, [PIECE * (h - s) for h in range(8)])
    x = lax.rem(column, 4)
    row_ref[...] = jnp.zeros(row_ref.shape, jnp.float32)
    faces = SIDE * PL_DEV
    for step, rows in ((0, damp_ref[...]), (1, right_ref[faces:, :]), (2, across_ref[...]), (3, left_ref[faces:, :])):
        row_ref[pl.ds(pl.multiple_of(lax.rem(x + step, 4) * PADDED, 8), NODES), :] = rows[:NODES]


def product(table_refs, x):
    high, low = table_refs
    xh, xl = split(x)
    return dot(high[...], xh) + (dot(high[...], xl) + dot(low[...], xh))


def forward_kernel(x_ref, high_ref, low_ref, out_ref):
    table = (high_ref, low_ref)
    for start in range(0, GROUPS, 2):
        x = jnp.concatenate(
            [
                jnp.concatenate([x_ref[s, g * PL_DEV : (g + 1) * PL_DEV, :] for s in range(N_SPAN)], axis=0)
                for g in (start, start + 1)
            ],
            axis=1,
        )
        res = product(table, x)
        for g in range(2):
            for j in range(M_DEV):
                out_ref[pl.ds(j * GROUPS + start + g, N_DEV, stride=PAIR), :] = res[
                    j * N_DEV : (j + 1) * N_DEV, g * EY : (g + 1) * EY
                ]
    packed = [x_ref[s, GROUPS * PL_DEV :, :] for s in range(N_SPAN)]
    x = jnp.concatenate([turn(packed[s], -PIECE * h) for s in range(N_SPAN) for h in range(8)], axis=0)
    res = product(table, x)
    parts = [res[j * N_DEV : (j + 1) * N_DEV] for j in range(M_DEV)]
    out_ref[pl.ds(PAIR - 1, N_DEV, stride=PAIR), :] = pack(parts, [PIECE * j for j in range(M_DEV)])


def inverse_kernel(x_ref, high_ref, low_ref, out_ref):
    table = (high_ref, low_ref)
    for start in range(0, GROUPS, 2):
        x = jnp.concatenate(
            [
                jnp.concatenate(
                    [x_ref[pl.ds(j * GROUPS + g, N_DEV, stride=PAIR), :] for j in range(M_DEV)], axis=0
                )
                for g in (start, start + 1)
            ],
            axis=1,
        )
        res = product(table, x)
        for g in range(2):
            for s in range(N_SPAN):
                out_ref[s, (start + g) * PL_DEV : (start + g + 1) * PL_DEV, :] = res[
                    s * PL_DEV : (s + 1) * PL_DEV, g * EY : (g + 1) * EY
                ]
    rest = x_ref[pl.ds(PAIR - 1, N_DEV, stride=PAIR), :]
    x = jnp.concatenate([turn(rest, -PIECE * j) for j in range(M_DEV)], axis=0)
    res = product(table, x)
    for s in range(N_SPAN):
        blocks = [res[s * PL_DEV + 8 * h : s * PL_DEV + 8 * h + 8] for h in range(8)]
        out_ref[s, GROUPS * PL_DEV :, :] = pack(blocks, [PIECE * h for h in range(8)])


def final_kernel(x_ref, out_ref):
    for s in range(N_SPAN):
        for g in range(GROUPS):
            out_ref[s * GROUPS + g] = x_ref[s, g * PL_DEV : (g + 1) * PL_DEV, :]
    packed = [x_ref[s, GROUPS * PL_DEV :, :] for s in range(N_SPAN)]
    for h in range(8):
        out_ref[NODES - 1, 8 * h : 8 * h + 8, :] = pack(packed, [PIECE * (s - h) for s in range(N_SPAN)])


def solve_tables():
    own = D.T @ np.diag(W) @ D
    own[6, 6] += PENALTY
    own[6, :] -= D[6, :] / 2
    own[:, 6] -= D[6, :] / 2
    own[0, 0] += PENALTY
    own[0, :] += D[0, :] / 2
    own[:, 0] += D[0, :] / 2
    return own


OWN = solve_tables()


def line_image(v, weight, from_next, from_before):
    own, d6, penalty = OWN * weight, D[6] * weight, np.float32(PENALTY * weight)
    even = [v[0] + v[6], v[1] + v[5], v[2] + v[4], v[3]]
    odd = [v[0] - v[6], v[1] - v[5], v[2] - v[4]]
    d_even = [(d6[a] + d6[6 - a]) / 2 for a in range(3)] + [d6[3]]
    d_odd = [(d6[a] - d6[6 - a]) / 2 for a in range(3)]
    half_even = combine([c / 2 for c in d_even], even)
    half_odd = combine([c / 2 for c in d_odd], odd)
    first = penalty * v[0] + (half_odd - half_even)
    last = penalty * v[6] - (half_even + half_odd)
    next_value = from_next(v[0])
    next_first = from_next(first)
    before_value = from_before(v[6])
    before_last = from_before(last)
    sum_value = next_value + before_value
    dif_value = next_value - before_value
    out = [None] * SIDE
    for i in range(3):
        e = combine(
            [(own[i, a] + own[i, 6 - a]) / 2 for a in range(3)] + [own[i, 3], d_even[i] / 2],
            even + [sum_value],
        )
        o = combine(
            [(own[i, a] - own[i, 6 - a]) / 2 for a in range(3)] + [d_odd[i] / 2],
            odd + [dif_value],
        )
        out[i] = e + o
        out[6 - i] = e - o
    out[3] = combine([own[3, a] for a in range(4)] + [d6[3] / 2], even + [sum_value])
    out[6] = out[6] - next_first
    out[0] = out[0] - before_last
    return out


def whole_sum(x):
    return jnp.sum(jnp.sum(x, axis=0, keepdims=True), axis=1, keepdims=True)


def solve_kernel(
    shift_ref, idle_ref, place_ref, b_ref, damp_ref, out_ref, mass_ref, x_ref, r_ref, p_ref, q_ref, ratio_ref, part_ref
):
    stride = N_SPAN * PAIR
    piece = piece_of((COLS, EY))
    half = COLS // 2
    column = lax.broadcasted_iota(jnp.int32, (half, EY), 0)
    zero = jnp.zeros((COLS, EY), jnp.float32)

    def load(ref, start, step):
        return jnp.concatenate(
            [ref[pl.ds(start, half, stride=2 * step), :], ref[pl.ds(start + step, half, stride=2 * step), :]],
            axis=0,
        )

    def store(start, step, value):
        out_ref[pl.ds(start, half, stride=2 * step), :] = value[:half]
        out_ref[pl.ds(start + step, half, stride=2 * step), :] = value[half:]

    def x_next(v):
        return jnp.concatenate(
            [v[half:], jnp.where(column < half - 1, pltpu.roll(v[:half], half - 1, 0), 0.0)], axis=0
        )

    def x_before(v):
        return jnp.concatenate([jnp.where(column > 0, pltpu.roll(v[half:], 1, 0), 0.0), v[:half]], axis=0)

    def y_next(v):
        return pltpu.roll(v, EY - 1, 1)

    def y_before(v):
        return pltpu.roll(v, 1, 1)

    def totals():
        return [whole_sum(part_ref[mode]) for mode in range(M_DEV)]

    place = lax.rem(place_ref[0], 4)
    wrap_odd = jnp.logical_and(place == 0, column % 2 == 1)
    wrap_even = jnp.logical_and(place == 3, column % 2 == 0)

    def damp_of(n):
        even = damp_ref[pl.ds(n, half, stride=2 * PADDED), :]
        odd = damp_ref[pl.ds(n + PADDED, half, stride=2 * PADDED), :]
        even = jnp.where(wrap_even, pltpu.roll(even, 2, 0), even)
        odd = jnp.where(wrap_odd, pltpu.roll(odd, half - 2, 0), odd)
        return jnp.concatenate([even, odd], axis=0)

    def begin(mode, carry):
        shift = shift_ref[mode]
        base = mode * NODES
        norm = zero
        for n in range(NODES):
            w = np.float32(W[n // SIDE] * W[n % SIDE])
            if n < NODES - 1:
                start = n // GROUPS * PAIR + n % GROUPS
                rows = load(b_ref, start + mode * GROUPS, stride)
            else:
                rows = zero
                for s in range(N_SPAN):
                    rest = load(b_ref, s * PAIR + PAIR - 1, stride)
                    own = pltpu.roll(rest, lax.rem(s * PIECE + EY - mode * PIECE, EY), 1)
                    rows = jnp.where(piece == s, own, rows)
            damp = damp_of(n)
            rhs = w * rows
            r_ref[base + n] = rhs
            p_ref[base + n] = zero
            x_ref[base + n] = zero
            mass_ref[base + n] = w * (damp + shift)
            norm = norm + rhs * rhs
        part_ref[mode] = norm
        ratio_ref[mode] = zero
        return carry

    lax.fori_loop(0, M_DEV, begin, 0)

    def apply(mode, carry):
        base = mode * NODES
        ratio = ratio_ref[mode]
        for j in range(SIDE):
            line = []
            for i in range(SIDE):
                n = base + i * SIDE + j
                p = r_ref[n] + ratio * p_ref[n]
                p_ref[n] = p
                line.append(p)
            image = line_image(line, W[j], x_next, x_before)
            for i in range(SIDE):
                n = base + i * SIDE + j
                q_ref[n] = image[i] + mass_ref[n] * line[i]
        curve = zero
        for i in range(SIDE):
            line = [p_ref[base + i * SIDE + j] for j in range(SIDE)]
            image = line_image(line, W[i], y_next, y_before)
            for j in range(SIDE):
                n = base + i * SIDE + j
                q = q_ref[n] + image[j]
                q_ref[n] = q
                curve = curve + q * line[j]
        part_ref[mode] = curve
        return carry

    def update(mode, carry):
        base = mode * NODES
        alpha = ratio_ref[mode]
        fresh = zero
        for n in range(NODES):
            x_ref[base + n] = x_ref[base + n] + alpha * p_ref[base + n]
            r = r_ref[base + n] - alpha * q_ref[base + n]
            r_ref[base + n] = r
            fresh = fresh + r * r
        part_ref[mode] = fresh
        return carry

    def spread(values):
        for mode in range(M_DEV):
            ratio_ref[mode] = jnp.broadcast_to(values[mode], (COLS, EY))

    def iteration(step, norm):
        lax.fori_loop(0, M_DEV, apply, 0)
        curve = totals()
        spread([norm[m] / (curve[m] + idle_ref[m]) for m in range(M_DEV)])
        lax.fori_loop(0, M_DEV, update, 0)
        fresh = totals()
        spread([fresh[m] / (norm[m] + idle_ref[m]) for m in range(M_DEV)])
        return tuple(fresh)

    lax.fori_loop(0, ITERS, iteration, tuple(totals()))

    def finish(mode, carry):
        base = mode * NODES
        for n in range(NODES - 1):
            start = n // GROUPS * PAIR + n % GROUPS
            store(start + mode * GROUPS, stride, x_ref[base + n])
        return carry

    lax.fori_loop(0, M_DEV, finish, 0)
    for s in range(N_SPAN):
        own = zero
        for mode in range(M_DEV):
            rest = turn(x_ref[mode * NODES + NODES - 1], (mode - s) * PIECE)
            own = jnp.where(piece == mode, rest, own)
        store(s * PAIR + PAIR - 1, stride, own)


def f32(shape):
    return jax.ShapeDtypeStruct(shape, jnp.float32)


def call(kernel, shape, scratch=(), smem=0, n_in=0):
    full = pl.BlockSpec(memory_space=pltpu.VMEM)
    scalar = pl.BlockSpec(memory_space=pltpu.SMEM)
    many = isinstance(shape, list)
    return pl.pallas_call(
        kernel,
        out_shape=[f32(s) for s in shape] if many else f32(shape),
        in_specs=[scalar] * smem + [full] * n_in,
        out_specs=[full] * len(shape) if many else full,
        scratch_shapes=[pltpu.VMEM(s, jnp.float32) for s in scratch],
        compiler_params=pltpu.CompilerParams(vmem_limit_bytes=VMEM),
    )


def body(velocity_q, advecting, damping):
    columns = ("y", "x")
    span = ("z", "core")
    everyone = columns + span
    up = [(i, (i + 1) % COLS) for i in range(COLS)]
    down = [(j, i) for i, j in up]
    q_nodes = jnp.transpose(velocity_q, (1, 0, 2))
    a_nodes = jnp.transpose(advecting, (0, 2, 1, 3))
    blank = jnp.zeros((PADDED - NODES, EY), jnp.float32)

    def beside(face):
        return jnp.concatenate([face.reshape(SIDE * PL_DEV, EY), damping, blank])

    from_left = lax.ppermute(beside(q_nodes[NODES - SIDE :]), columns, up)
    from_right = lax.ppermute(beside(q_nodes[:SIDE]), columns, down)
    across = lax.ppermute(damping, "x", [(i, (i + 2) % 4) for i in range(4)])
    inner = call(inner_kernel, (NODES, PL_DEV, EY), n_in=2)(q_nodes, a_nodes)
    place = lax.axis_index(columns).astype(jnp.int32)[None]
    forcing, damp_row = call(
        outer_kernel, [(N_SPAN, ROWS, EY), (4 * PADDED, EY)], scratch=((PL_DEV, EY),), smem=1, n_in=6
    )(place, inner, from_left, from_right, across, damping, a_nodes)
    device = lax.axis_index(everyone)
    coef = device * M_DEV + jnp.arange(M_DEV, dtype=jnp.int32)
    wave = jnp.where(coef < WAVES, coef, coef - WAVES + 1).astype(jnp.float32)
    shifts = LAMBDA0 + (BETA * wave) ** 2
    idle = jnp.where(coef < KEPT, 0.0, 1.0).astype(jnp.float32)
    forcing, damp_row, shifts, idle = lax.optimization_barrier((forcing, damp_row, shifts, idle))
    planes = lax.all_to_all(forcing, span, split_axis=0, concat_axis=0, tiled=True)
    damp_nodes = lax.all_gather(damp_row, "y", axis=0, tiled=True)
    planes, damp_nodes = lax.optimization_barrier((planes, damp_nodes))

    forward, backward = fourier_table()
    spectra = call(forward_kernel, (N_DEV * PAIR, EY), n_in=3)(planes, *in_two(forward))
    mine = lax.all_to_all(
        spectra.reshape(N_DEV, 1, PAIR * EY), everyone, split_axis=0, concat_axis=0, tiled=True
    )

    field, part = (M_DEV * NODES, COLS, EY), (M_DEV, COLS, EY)
    solved = call(solve_kernel, (N_DEV * PAIR, EY), scratch=(field,) * 5 + (part,) * 2, smem=3, n_in=2)(
        shifts, idle, place, mine.reshape(N_DEV * PAIR, EY), damp_nodes
    )

    modes = lax.all_to_all(
        solved.reshape(N_DEV, 1, PAIR * EY), everyone, split_axis=0, concat_axis=0, tiled=True
    )
    physical = call(inverse_kernel, (N_SPAN, ROWS, EY), n_in=3)(
        modes.reshape(N_DEV * PAIR, EY), *in_two(backward)
    )
    back = lax.all_to_all(physical, span, split_axis=0, concat_axis=0, tiled=True)
    q_new = call(final_kernel, (NODES, PL_DEV, EY), n_in=1)(back)
    return jnp.transpose(q_new, (1, 0, 2))


def solution(mesh):
    columns, span = ("y", "x"), ("z", "core")
    side = math.isqrt(COLS)
    parts = Mesh(mesh.devices.reshape(side, side, N_SPAN // 2, 2), columns + span)
    placed = (P(span, None, columns), P(None, span, None, columns), P(None, columns))
    return jax.shard_map(
        body, mesh=parts, in_specs=placed, out_specs=P(span, None, columns), check_vma=False
    )
```

```python
import math

import jax
import jax.numpy as jnp
import ml_dtypes
import numpy as np
from jax import lax
from jax.experimental import pallas as pl
from jax.experimental.pallas import tpu as pltpu
from jax.sharding import Mesh, PartitionSpec as P

ORDER = 6
SIDE = 7
NODES = 49
EY = 128
COLS = 16
PLANES = 512
PL_DEV = 64
N_SPAN = 8
N_DEV = 128
WAVES = 168
KEPT = 336
M_DEV = 3
M_ALL = N_DEV * M_DEV
GROUPS = 6
PIECE = 16
ROWS = GROUPS * PL_DEV + 8
PAIR = GROUPS * M_DEV + 1
PADDED = 56
ITERS = 8

LAMBDA0 = 0.1
VISCOSITY = 0.02
PENALTY = 100.0
BETA = 0.02
VMEM = 16 * 1024 * 1024


def gll_tables(degree):
    side_nodes = degree + 1
    points = [-math.cos(math.pi * n / degree) for n in range(side_nodes)]
    values = [1.0] * side_nodes
    for _ in range(60):
        updated = []
        new_values = []
        for point in points:
            lower = 1.0
            now = point
            for step in range(2, degree + 1):
                lower, now = now, ((2 * step - 1) * point * now - (step - 1) * lower) / step
            updated.append(point - (point * now - lower) / (side_nodes * now))
            new_values.append(now)
        points = updated
        values = new_values
    weights = np.array([2.0 / (degree * side_nodes * v * v) for v in values])
    derivative = np.zeros((side_nodes, side_nodes))
    for row in range(side_nodes):
        for col in range(side_nodes):
            if row != col:
                derivative[row, col] = values[row] / (values[col] * (points[row] - points[col]))
    derivative[0, 0] = -degree * side_nodes / 4.0
    derivative[degree, degree] = degree * side_nodes / 4.0
    return weights, derivative


W, D = gll_tables(ORDER)
EDGE = 1.0 / (2.0 * W[0] * VISCOSITY)


def fourier_table():
    row = np.arange(M_ALL)[:, None]
    c = row % N_DEV * M_DEV + row // N_DEV
    p = np.arange(PLANES)[None, :]
    k = np.where(c < WAVES, c, c - WAVES + 1)
    phases = ((k * p) % PLANES) * (2.0 * math.pi / PLANES)
    table = np.where(c < WAVES, np.cos(phases), np.sin(phases))
    scale = np.where(c == 0, 1.0 / PLANES, 2.0 / PLANES)
    table = np.where(c < KEPT, table, 0.0)
    return table * scale, table.T


def in_two(table):
    table = table.astype(np.float32)
    high = table.astype(ml_dtypes.bfloat16)
    low = (table - high.astype(np.float32)).astype(ml_dtypes.bfloat16)
    return jnp.asarray(high), jnp.asarray(low)


def split(x):
    high = x.astype(jnp.bfloat16)
    low = (x - high.astype(jnp.float32)).astype(jnp.bfloat16)
    return high, low


def dot(a, b):
    return jnp.dot(a, b, preferred_element_type=jnp.float32)


def combine(coefs, values):
    total = None
    for c, v in zip(coefs, values):
        if c == 0.0:
            continue
        term = v * np.float32(c)
        total = term if total is None else total + term
    return total


def turn(x, by):
    by = by % EY
    return pltpu.roll(x, by, 1) if by else x


def piece_of(shape):
    return lax.broadcasted_iota(jnp.int32, shape, 1) // PIECE


def pack(blocks, turns):
    piece = piece_of(blocks[0].shape)
    out = turn(blocks[0], turns[0])
    for h in range(1, len(blocks)):
        out = jnp.where(piece == h, turn(blocks[h], turns[h]), out)
    return out


def inner_kernel(q_ref, a_ref, out_ref):
    table = D / VISCOSITY
    own = table.copy()
    own[6, 6] -= EDGE
    own[0, 0] += EDGE
    edge = np.float32(EDGE)

    def block(b, carry):
        rows = pl.ds(pl.multiple_of(b * 16, 16), 16)
        for i in range(SIDE):
            line = [q_ref[i * SIDE + j, rows, :] for j in range(SIDE)]
            gy = [combine(own[j], line) for j in range(SIDE)]
            gy[6] = gy[6] + edge * pltpu.roll(line[0], EY - 1, 1)
            gy[0] = gy[0] - edge * pltpu.roll(line[6], 1, 1)
            for j in range(SIDE):
                n = i * SIDE + j
                gx = combine(own[i], [q_ref[a * SIDE + j, rows, :] for a in range(SIDE)])
                ax = a_ref[0, n, rows, :].astype(jnp.float32)
                ay = a_ref[1, n, rows, :].astype(jnp.float32)
                out_ref[n, rows, :] = np.float32(LAMBDA0) * line[j] - (ax * gx + ay * gy[j])
        return carry

    lax.fori_loop(0, PL_DEV // 16, block, 0)


def outer_kernel(
    place_ref, inner_ref, left_ref, right_ref, across_ref, damp_ref, a_ref, out_ref, row_ref, last_ref
):
    column = place_ref[0]
    has_left = jnp.where(column > 0, 1.0, 0.0)
    has_right = jnp.where(column < COLS - 1, 1.0, 0.0)
    edge = np.float32(EDGE)
    for n in range(NODES):
        target = last_ref if n == NODES - 1 else out_ref.at[n // GROUPS]
        start = 0 if n == NODES - 1 else n % GROUPS * PL_DEV
        j = n % SIDE
        face = slice(j * PL_DEV, (j + 1) * PL_DEV)
        value = inner_ref[n]
        if n < SIDE:
            value = value + (edge * has_left) * left_ref[face, :] * a_ref[0, n].astype(jnp.float32)
        if n >= NODES - SIDE:
            value = value - (edge * has_right) * right_ref[face, :] * a_ref[0, n].astype(jnp.float32)
        target[start : start + PL_DEV, :] = value
    for s in range(N_SPAN):
        blocks = [last_ref[8 * h : 8 * h + 8, :] for h in range(8)]
        out_ref[s, GROUPS * PL_DEV :, :] = pack(blocks, [PIECE * (h - s) for h in range(8)])
    x = lax.rem(column, 4)
    row_ref[...] = jnp.zeros(row_ref.shape, jnp.float32)
    faces = SIDE * PL_DEV
    for step, rows in ((0, damp_ref[...]), (1, right_ref[faces:, :]), (2, across_ref[...]), (3, left_ref[faces:, :])):
        row_ref[pl.ds(pl.multiple_of(lax.rem(x + step, 4) * PADDED, 8), NODES), :] = rows[:NODES]


def product(table_refs, x):
    high, low = table_refs
    xh, xl = split(x)
    return dot(high[...], xh) + (dot(high[...], xl) + dot(low[...], xh))


def forward_kernel(x_ref, high_ref, low_ref, out_ref):
    table = (high_ref, low_ref)
    for start in range(0, GROUPS, 2):
        x = jnp.concatenate(
            [
                jnp.concatenate([x_ref[s, g * PL_DEV : (g + 1) * PL_DEV, :] for s in range(N_SPAN)], axis=0)
                for g in (start, start + 1)
            ],
            axis=1,
        )
        res = product(table, x)
        for g in range(2):
            for j in range(M_DEV):
                out_ref[pl.ds(j * GROUPS + start + g, N_DEV, stride=PAIR), :] = res[
                    j * N_DEV : (j + 1) * N_DEV, g * EY : (g + 1) * EY
                ]
    packed = [x_ref[s, GROUPS * PL_DEV :, :] for s in range(N_SPAN)]
    x = jnp.concatenate([turn(packed[s], -PIECE * h) for s in range(N_SPAN) for h in range(8)], axis=0)
    res = product(table, x)
    parts = [res[j * N_DEV : (j + 1) * N_DEV] for j in range(M_DEV)]
    out_ref[pl.ds(PAIR - 1, N_DEV, stride=PAIR), :] = pack(parts, [PIECE * j for j in range(M_DEV)])


def inverse_kernel(x_ref, high_ref, low_ref, out_ref):
    table = (high_ref, low_ref)
    for start in range(0, GROUPS, 2):
        x = jnp.concatenate(
            [
                jnp.concatenate(
                    [x_ref[pl.ds(j * GROUPS + g, N_DEV, stride=PAIR), :] for j in range(M_DEV)], axis=0
                )
                for g in (start, start + 1)
            ],
            axis=1,
        )
        res = product(table, x)
        for g in range(2):
            for s in range(N_SPAN):
                out_ref[s, (start + g) * PL_DEV : (start + g + 1) * PL_DEV, :] = res[
                    s * PL_DEV : (s + 1) * PL_DEV, g * EY : (g + 1) * EY
                ]
    rest = x_ref[pl.ds(PAIR - 1, N_DEV, stride=PAIR), :]
    x = jnp.concatenate([turn(rest, -PIECE * j) for j in range(M_DEV)], axis=0)
    res = product(table, x)
    for s in range(N_SPAN):
        blocks = [res[s * PL_DEV + 8 * h : s * PL_DEV + 8 * h + 8] for h in range(8)]
        out_ref[s, GROUPS * PL_DEV :, :] = pack(blocks, [PIECE * h for h in range(8)])


def final_kernel(x_ref, out_ref):
    for s in range(N_SPAN):
        for g in range(GROUPS):
            out_ref[s * GROUPS + g] = x_ref[s, g * PL_DEV : (g + 1) * PL_DEV, :]
    packed = [x_ref[s, GROUPS * PL_DEV :, :] for s in range(N_SPAN)]
    for h in range(8):
        out_ref[NODES - 1, 8 * h : 8 * h + 8, :] = pack(packed, [PIECE * (s - h) for s in range(N_SPAN)])


def solve_tables():
    own = D.T @ np.diag(W) @ D
    own[6, 6] += PENALTY
    own[6, :] -= D[6, :] / 2
    own[:, 6] -= D[6, :] / 2
    own[0, 0] += PENALTY
    own[0, :] += D[0, :] / 2
    own[:, 0] += D[0, :] / 2
    return own


OWN = solve_tables()


def line_image(v, weight, from_next, from_before):
    own, d6, penalty = OWN * weight, D[6] * weight, np.float32(PENALTY * weight)
    even = [v[0] + v[6], v[1] + v[5], v[2] + v[4], v[3]]
    odd = [v[0] - v[6], v[1] - v[5], v[2] - v[4]]
    d_even = [(d6[a] + d6[6 - a]) / 2 for a in range(3)] + [d6[3]]
    d_odd = [(d6[a] - d6[6 - a]) / 2 for a in range(3)]
    half_even = combine([c / 2 for c in d_even], even)
    half_odd = combine([c / 2 for c in d_odd], odd)
    first = penalty * v[0] + (half_odd - half_even)
    last = penalty * v[6] - (half_even + half_odd)
    next_value = from_next(v[0])
    next_first = from_next(first)
    before_value = from_before(v[6])
    before_last = from_before(last)
    sum_value = next_value + before_value
    dif_value = next_value - before_value
    out = [None] * SIDE
    for i in range(3):
        e = combine(
            [(own[i, a] + own[i, 6 - a]) / 2 for a in range(3)] + [own[i, 3], d_even[i] / 2],
            even + [sum_value],
        )
        o = combine(
            [(own[i, a] - own[i, 6 - a]) / 2 for a in range(3)] + [d_odd[i] / 2],
            odd + [dif_value],
        )
        out[i] = e + o
        out[6 - i] = e - o
    out[3] = combine([own[3, a] for a in range(4)] + [d6[3] / 2], even + [sum_value])
    out[6] = out[6] - next_first
    out[0] = out[0] - before_last
    return out


def first_row(s):
    return (s % 2 * (N_SPAN // 2) + s // 2) * COLS * PAIR


def whole_sum(x):
    return jnp.sum(jnp.sum(x, axis=0, keepdims=True), axis=1, keepdims=True)


def solve_kernel(
    shift_ref, idle_ref, place_ref, b_ref, damp_ref, out_ref, mass_ref, x_ref, r_ref, p_ref, q_ref, ratio_ref, part_ref
):
    stride = PAIR
    piece = piece_of((COLS, EY))
    half = COLS // 2
    column = lax.broadcasted_iota(jnp.int32, (half, EY), 0)
    zero = jnp.zeros((COLS, EY), jnp.float32)

    def load(ref, start, step):
        return jnp.concatenate(
            [ref[pl.ds(start, half, stride=2 * step), :], ref[pl.ds(start + step, half, stride=2 * step), :]],
            axis=0,
        )

    def store(start, step, value):
        out_ref[pl.ds(start, half, stride=2 * step), :] = value[:half]
        out_ref[pl.ds(start + step, half, stride=2 * step), :] = value[half:]

    def x_next(v):
        return jnp.concatenate(
            [v[half:], jnp.where(column < half - 1, pltpu.roll(v[:half], half - 1, 0), 0.0)], axis=0
        )

    def x_before(v):
        return jnp.concatenate([jnp.where(column > 0, pltpu.roll(v[half:], 1, 0), 0.0), v[:half]], axis=0)

    def y_next(v):
        return pltpu.roll(v, EY - 1, 1)

    def y_before(v):
        return pltpu.roll(v, 1, 1)

    def totals():
        return [whole_sum(part_ref[mode]) for mode in range(M_DEV)]

    place = lax.rem(place_ref[0], 4)
    wrap_odd = jnp.logical_and(place == 0, column % 2 == 1)
    wrap_even = jnp.logical_and(place == 3, column % 2 == 0)

    def damp_of(n):
        even = damp_ref[pl.ds(n, half, stride=2 * PADDED), :]
        odd = damp_ref[pl.ds(n + PADDED, half, stride=2 * PADDED), :]
        even = jnp.where(wrap_even, pltpu.roll(even, 2, 0), even)
        odd = jnp.where(wrap_odd, pltpu.roll(odd, half - 2, 0), odd)
        return jnp.concatenate([even, odd], axis=0)

    def begin(mode, carry):
        shift = shift_ref[mode]
        base = mode * NODES
        norm = zero
        for n in range(NODES):
            w = np.float32(W[n // SIDE] * W[n % SIDE])
            if n < NODES - 1:
                start = first_row(n // GROUPS) + n % GROUPS
                rows = load(b_ref, start + mode * GROUPS, stride)
            else:
                rows = zero
                for s in range(N_SPAN):
                    rest = load(b_ref, first_row(s) + PAIR - 1, stride)
                    own = pltpu.roll(rest, lax.rem(s * PIECE + EY - mode * PIECE, EY), 1)
                    rows = jnp.where(piece == s, own, rows)
            damp = damp_of(n)
            rhs = w * rows
            r_ref[base + n] = rhs
            p_ref[base + n] = zero
            x_ref[base + n] = zero
            mass_ref[base + n] = w * (damp + shift)
            norm = norm + rhs * rhs
        part_ref[mode] = norm
        ratio_ref[mode] = zero
        return carry

    lax.fori_loop(0, M_DEV, begin, 0)

    def apply(mode, carry):
        base = mode * NODES
        ratio = ratio_ref[mode]
        for j in range(SIDE):
            line = []
            for i in range(SIDE):
                n = base + i * SIDE + j
                p = r_ref[n] + ratio * p_ref[n]
                p_ref[n] = p
                line.append(p)
            image = line_image(line, W[j], x_next, x_before)
            for i in range(SIDE):
                n = base + i * SIDE + j
                q_ref[n] = image[i] + mass_ref[n] * line[i]
        curve = zero
        for i in range(SIDE):
            line = [p_ref[base + i * SIDE + j] for j in range(SIDE)]
            image = line_image(line, W[i], y_next, y_before)
            for j in range(SIDE):
                n = base + i * SIDE + j
                q = q_ref[n] + image[j]
                q_ref[n] = q
                curve = curve + q * line[j]
        part_ref[mode] = curve
        return carry

    def update(mode, carry):
        base = mode * NODES
        alpha = ratio_ref[mode]
        fresh = zero
        for n in range(NODES):
            x_ref[base + n] = x_ref[base + n] + alpha * p_ref[base + n]
            r = r_ref[base + n] - alpha * q_ref[base + n]
            r_ref[base + n] = r
            fresh = fresh + r * r
        part_ref[mode] = fresh
        return carry

    def spread(values):
        for mode in range(M_DEV):
            ratio_ref[mode] = jnp.broadcast_to(values[mode], (COLS, EY))

    def iteration(step, norm):
        lax.fori_loop(0, M_DEV, apply, 0)
        curve = totals()
        spread([norm[m] / (curve[m] + idle_ref[m]) for m in range(M_DEV)])
        for mode in range(M_DEV):
            update(mode, 0)
        fresh = totals()
        spread([fresh[m] / (norm[m] + idle_ref[m]) for m in range(M_DEV)])
        return tuple(fresh)

    lax.fori_loop(0, ITERS, iteration, tuple(totals()))

    def finish(mode, carry):
        base = mode * NODES
        for n in range(NODES - 1):
            start = first_row(n // GROUPS) + n % GROUPS
            store(start + mode * GROUPS, stride, x_ref[base + n])
        return carry

    lax.fori_loop(0, M_DEV, finish, 0)
    for s in range(N_SPAN):
        own = zero
        for mode in range(M_DEV):
            rest = turn(x_ref[mode * NODES + NODES - 1], (mode - s) * PIECE)
            own = jnp.where(piece == mode, rest, own)
        store(first_row(s) + PAIR - 1, stride, own)


def f32(shape):
    return jax.ShapeDtypeStruct(shape, jnp.float32)


def call(kernel, shape, scratch=(), smem=0, n_in=0):
    full = pl.BlockSpec(memory_space=pltpu.VMEM)
    scalar = pl.BlockSpec(memory_space=pltpu.SMEM)
    many = isinstance(shape, list)
    return pl.pallas_call(
        kernel,
        out_shape=[f32(s) for s in shape] if many else f32(shape),
        in_specs=[scalar] * smem + [full] * n_in,
        out_specs=[full] * len(shape) if many else full,
        scratch_shapes=[pltpu.VMEM(s, jnp.float32) for s in scratch],
        compiler_params=pltpu.CompilerParams(vmem_limit_bytes=VMEM),
    )


def body(velocity_q, advecting, damping):
    columns = ("y", "x")
    span = ("z", "core")
    everyone = ("core", "z") + columns
    up = [(i, (i + 1) % COLS) for i in range(COLS)]
    down = [(j, i) for i, j in up]
    q_nodes = jnp.transpose(velocity_q, (1, 0, 2))
    a_nodes = jnp.transpose(advecting, (0, 2, 1, 3))
    blank = jnp.zeros((PADDED - NODES, EY), jnp.float32)

    def beside(face):
        return jnp.concatenate([face.reshape(SIDE * PL_DEV, EY), damping, blank])

    from_left = lax.ppermute(beside(q_nodes[NODES - SIDE :]), columns, up)
    from_right = lax.ppermute(beside(q_nodes[:SIDE]), columns, down)
    across = lax.ppermute(damping, "x", [(i, (i + 2) % 4) for i in range(4)])
    inner = call(inner_kernel, (NODES, PL_DEV, EY), n_in=2)(q_nodes, a_nodes)
    place = lax.axis_index(columns).astype(jnp.int32)[None]
    forcing, damp_row = call(
        outer_kernel, [(N_SPAN, ROWS, EY), (4 * PADDED, EY)], scratch=((PL_DEV, EY),), smem=1, n_in=6
    )(place, inner, from_left, from_right, across, damping, a_nodes)
    device = lax.axis_index(everyone)
    coef = device * M_DEV + jnp.arange(M_DEV, dtype=jnp.int32)
    wave = jnp.where(coef < WAVES, coef, coef - WAVES + 1).astype(jnp.float32)
    shifts = LAMBDA0 + (BETA * wave) ** 2
    idle = jnp.where(coef < KEPT, 0.0, 1.0).astype(jnp.float32)
    forcing, damp_row, shifts, idle = lax.optimization_barrier((forcing, damp_row, shifts, idle))
    planes = lax.all_to_all(forcing, span, split_axis=0, concat_axis=0, tiled=True)
    damp_nodes = lax.all_gather(damp_row, "y", axis=0, tiled=True)
    planes, damp_nodes = lax.optimization_barrier((planes, damp_nodes))

    forward, backward = fourier_table()
    spectra = call(forward_kernel, (N_DEV * PAIR, EY), n_in=3)(planes, *in_two(forward))
    mine = lax.all_to_all(
        spectra.reshape(N_DEV, 1, PAIR * EY), everyone, split_axis=0, concat_axis=0, tiled=True
    )

    field, part = (M_DEV * NODES, COLS, EY), (M_DEV, COLS, EY)
    solved = call(solve_kernel, (N_DEV * PAIR, EY), scratch=(field,) * 5 + (part,) * 2, smem=3, n_in=2)(
        shifts, idle, place, mine.reshape(N_DEV * PAIR, EY), damp_nodes
    )

    modes = lax.all_to_all(
        solved.reshape(N_DEV, 1, PAIR * EY), everyone, split_axis=0, concat_axis=0, tiled=True
    )
    physical = call(inverse_kernel, (N_SPAN, ROWS, EY), n_in=3)(
        modes.reshape(N_DEV * PAIR, EY), *in_two(backward)
    )
    back = lax.all_to_all(physical, span, split_axis=0, concat_axis=0, tiled=True)
    q_new = call(final_kernel, (NODES, PL_DEV, EY), n_in=1)(back)
    return jnp.transpose(q_new, (1, 0, 2))


def solution(mesh):
    columns, span = ("y", "x"), ("z", "core")
    side = math.isqrt(COLS)
    parts = Mesh(mesh.devices.reshape(side, side, N_SPAN // 2, 2), columns + span)
    placed = (P(span, None, columns), P(None, span, None, columns), P(None, columns))
    return jax.shard_map(
        body, mesh=parts, in_specs=placed, out_specs=P(span, None, columns), check_vma=False
    )
```

```python
import math

import jax
import jax.numpy as jnp
import ml_dtypes
import numpy as np
from jax import lax
from jax.experimental import pallas as pl
from jax.experimental.pallas import tpu as pltpu
from jax.sharding import Mesh, PartitionSpec as P

ORDER = 6
SIDE = 7
NODES = 49
EY = 128
COLS = 16
PLANES = 512
PL_DEV = 64
N_SPAN = 8
N_DEV = 128
WAVES = 168
KEPT = 336
M_DEV = 3
M_ALL = N_DEV * M_DEV
GROUPS = 6
PIECE = 16
ROWS = GROUPS * PL_DEV + 8
PAIR = GROUPS * M_DEV + 1
PADDED = 56
ITERS = 8

LAMBDA0 = 0.1
VISCOSITY = 0.02
PENALTY = 100.0
BETA = 0.02
VMEM = 16 * 1024 * 1024


def gll_tables(degree):
    side_nodes = degree + 1
    points = [-math.cos(math.pi * n / degree) for n in range(side_nodes)]
    values = [1.0] * side_nodes
    for _ in range(60):
        updated = []
        new_values = []
        for point in points:
            lower = 1.0
            now = point
            for step in range(2, degree + 1):
                lower, now = now, ((2 * step - 1) * point * now - (step - 1) * lower) / step
            updated.append(point - (point * now - lower) / (side_nodes * now))
            new_values.append(now)
        points = updated
        values = new_values
    weights = np.array([2.0 / (degree * side_nodes * v * v) for v in values])
    derivative = np.zeros((side_nodes, side_nodes))
    for row in range(side_nodes):
        for col in range(side_nodes):
            if row != col:
                derivative[row, col] = values[row] / (values[col] * (points[row] - points[col]))
    derivative[0, 0] = -degree * side_nodes / 4.0
    derivative[degree, degree] = degree * side_nodes / 4.0
    return weights, derivative


W, D = gll_tables(ORDER)
EDGE = 1.0 / (2.0 * W[0] * VISCOSITY)


def fourier_table():
    row = np.arange(M_ALL)[:, None]
    c = row % N_DEV * M_DEV + row // N_DEV
    p = np.arange(PLANES)[None, :]
    k = np.where(c < WAVES, c, c - WAVES + 1)
    phases = ((k * p) % PLANES) * (2.0 * math.pi / PLANES)
    table = np.where(c < WAVES, np.cos(phases), np.sin(phases))
    scale = np.where(c == 0, 1.0 / PLANES, 2.0 / PLANES)
    table = np.where(c < KEPT, table, 0.0)
    return table * scale, table.T


def in_two(table):
    table = table.astype(np.float32)
    high = table.astype(ml_dtypes.bfloat16)
    low = (table - high.astype(np.float32)).astype(ml_dtypes.bfloat16)
    return jnp.asarray(high), jnp.asarray(low)


def split(x):
    high = x.astype(jnp.bfloat16)
    low = (x - high.astype(jnp.float32)).astype(jnp.bfloat16)
    return high, low


def dot(a, b):
    return jnp.dot(a, b, preferred_element_type=jnp.float32)


def combine(coefs, values):
    total = None
    for c, v in zip(coefs, values):
        if c == 0.0:
            continue
        term = v * np.float32(c)
        total = term if total is None else total + term
    return total


def turn(x, by):
    by = by % EY
    return pltpu.roll(x, by, 1) if by else x


def piece_of(shape):
    return lax.broadcasted_iota(jnp.int32, shape, 1) // PIECE


def pack(blocks, turns):
    piece = piece_of(blocks[0].shape)
    out = turn(blocks[0], turns[0])
    for h in range(1, len(blocks)):
        out = jnp.where(piece == h, turn(blocks[h], turns[h]), out)
    return out


def inner_kernel(q_ref, a_ref, out_ref):
    table = D / VISCOSITY
    own = table.copy()
    own[6, 6] -= EDGE
    own[0, 0] += EDGE
    edge = np.float32(EDGE)

    def block(b, carry):
        rows = pl.ds(pl.multiple_of(b * 16, 16), 16)
        for i in range(SIDE):
            line = [q_ref[i * SIDE + j, rows, :] for j in range(SIDE)]
            gy = [combine(own[j], line) for j in range(SIDE)]
            gy[6] = gy[6] + edge * pltpu.roll(line[0], EY - 1, 1)
            gy[0] = gy[0] - edge * pltpu.roll(line[6], 1, 1)
            for j in range(SIDE):
                n = i * SIDE + j
                gx = combine(own[i], [q_ref[a * SIDE + j, rows, :] for a in range(SIDE)])
                ax = a_ref[0, n, rows, :].astype(jnp.float32)
                ay = a_ref[1, n, rows, :].astype(jnp.float32)
                out_ref[n, rows, :] = np.float32(LAMBDA0) * line[j] - (ax * gx + ay * gy[j])
        return carry

    lax.fori_loop(0, PL_DEV // 16, block, 0)


def outer_kernel(
    place_ref, inner_ref, left_ref, right_ref, across_ref, damp_ref, a_ref, out_ref, row_ref, last_ref
):
    column = place_ref[0]
    has_left = jnp.where(column > 0, 1.0, 0.0)
    has_right = jnp.where(column < COLS - 1, 1.0, 0.0)
    edge = np.float32(EDGE)
    for n in range(NODES):
        target = last_ref if n == NODES - 1 else out_ref.at[n // GROUPS]
        start = 0 if n == NODES - 1 else n % GROUPS * PL_DEV
        j = n % SIDE
        face = slice(j * PL_DEV, (j + 1) * PL_DEV)
        value = inner_ref[n]
        if n < SIDE:
            value = value + (edge * has_left) * left_ref[face, :] * a_ref[0, n].astype(jnp.float32)
        if n >= NODES - SIDE:
            value = value - (edge * has_right) * right_ref[face, :] * a_ref[0, n].astype(jnp.float32)
        target[start : start + PL_DEV, :] = value
    for s in range(N_SPAN):
        blocks = [last_ref[8 * h : 8 * h + 8, :] for h in range(8)]
        out_ref[s, GROUPS * PL_DEV :, :] = pack(blocks, [PIECE * (h - s) for h in range(8)])
    x = lax.rem(column, 4)
    row_ref[...] = jnp.zeros(row_ref.shape, jnp.float32)
    faces = SIDE * PL_DEV
    for step, rows in ((0, damp_ref[...]), (1, right_ref[faces:, :]), (2, across_ref[...]), (3, left_ref[faces:, :])):
        row_ref[pl.ds(pl.multiple_of(lax.rem(x + step, 4) * PADDED, 8), NODES), :] = rows[:NODES]


def product(table_refs, x):
    high, low = table_refs
    xh, xl = split(x)
    return dot(high[...], xh) + (dot(high[...], xl) + dot(low[...], xh))


def forward_kernel(x_ref, high_ref, low_ref, out_ref):
    table = (high_ref, low_ref)
    for start in range(0, GROUPS, 2):
        x = jnp.concatenate(
            [
                jnp.concatenate([x_ref[s, g * PL_DEV : (g + 1) * PL_DEV, :] for s in range(N_SPAN)], axis=0)
                for g in (start, start + 1)
            ],
            axis=1,
        )
        res = product(table, x)
        for g in range(2):
            for j in range(M_DEV):
                out_ref[pl.ds(j * GROUPS + start + g, N_DEV, stride=PAIR), :] = res[
                    j * N_DEV : (j + 1) * N_DEV, g * EY : (g + 1) * EY
                ]
    packed = [x_ref[s, GROUPS * PL_DEV :, :] for s in range(N_SPAN)]
    x = jnp.concatenate([turn(packed[s], -PIECE * h) for s in range(N_SPAN) for h in range(8)], axis=0)
    res = product(table, x)
    parts = [res[j * N_DEV : (j + 1) * N_DEV] for j in range(M_DEV)]
    out_ref[pl.ds(PAIR - 1, N_DEV, stride=PAIR), :] = pack(parts, [PIECE * j for j in range(M_DEV)])


def inverse_kernel(x_ref, high_ref, low_ref, out_ref):
    table = (high_ref, low_ref)
    for start in range(0, GROUPS, 2):
        x = jnp.concatenate(
            [
                jnp.concatenate(
                    [x_ref[pl.ds(j * GROUPS + g, N_DEV, stride=PAIR), :] for j in range(M_DEV)], axis=0
                )
                for g in (start, start + 1)
            ],
            axis=1,
        )
        res = product(table, x)
        for g in range(2):
            for s in range(N_SPAN):
                out_ref[s, (start + g) * PL_DEV : (start + g + 1) * PL_DEV, :] = res[
                    s * PL_DEV : (s + 1) * PL_DEV, g * EY : (g + 1) * EY
                ]
    rest = x_ref[pl.ds(PAIR - 1, N_DEV, stride=PAIR), :]
    x = jnp.concatenate([turn(rest, -PIECE * j) for j in range(M_DEV)], axis=0)
    res = product(table, x)
    for s in range(N_SPAN):
        blocks = [res[s * PL_DEV + 8 * h : s * PL_DEV + 8 * h + 8] for h in range(8)]
        out_ref[s, GROUPS * PL_DEV :, :] = pack(blocks, [PIECE * h for h in range(8)])


def final_kernel(x_ref, out_ref):
    for s in range(N_SPAN):
        for g in range(GROUPS):
            out_ref[s * GROUPS + g] = x_ref[s, g * PL_DEV : (g + 1) * PL_DEV, :]
    packed = [x_ref[s, GROUPS * PL_DEV :, :] for s in range(N_SPAN)]
    for h in range(8):
        out_ref[NODES - 1, 8 * h : 8 * h + 8, :] = pack(packed, [PIECE * (s - h) for s in range(N_SPAN)])


def solve_tables():
    own = D.T @ np.diag(W) @ D
    own[6, 6] += PENALTY
    own[6, :] -= D[6, :] / 2
    own[:, 6] -= D[6, :] / 2
    own[0, 0] += PENALTY
    own[0, :] += D[0, :] / 2
    own[:, 0] += D[0, :] / 2
    return own


OWN = solve_tables()


def line_image(v, weight, from_next, from_before):
    own, d6, penalty = OWN * weight, D[6] * weight, np.float32(PENALTY * weight)
    even = [v[0] + v[6], v[1] + v[5], v[2] + v[4], v[3]]
    odd = [v[0] - v[6], v[1] - v[5], v[2] - v[4]]
    d_even = [(d6[a] + d6[6 - a]) / 2 for a in range(3)] + [d6[3]]
    d_odd = [(d6[a] - d6[6 - a]) / 2 for a in range(3)]
    half_even = combine([c / 2 for c in d_even], even)
    half_odd = combine([c / 2 for c in d_odd], odd)
    first = penalty * v[0] + (half_odd - half_even)
    last = penalty * v[6] - (half_even + half_odd)
    next_value = from_next(v[0])
    next_first = from_next(first)
    before_value = from_before(v[6])
    before_last = from_before(last)
    sum_value = next_value + before_value
    dif_value = next_value - before_value
    out = [None] * SIDE
    for i in range(3):
        e = combine(
            [(own[i, a] + own[i, 6 - a]) / 2 for a in range(3)] + [own[i, 3], d_even[i] / 2],
            even + [sum_value],
        )
        o = combine(
            [(own[i, a] - own[i, 6 - a]) / 2 for a in range(3)] + [d_odd[i] / 2],
            odd + [dif_value],
        )
        out[i] = e + o
        out[6 - i] = e - o
    out[3] = combine([own[3, a] for a in range(4)] + [d6[3] / 2], even + [sum_value])
    out[6] = out[6] - next_first
    out[0] = out[0] - before_last
    return out


def first_row(s):
    return (s % 2 * (N_SPAN // 2) + s // 2) * COLS * PAIR


def whole_sum(x):
    return jnp.sum(jnp.sum(x, axis=0, keepdims=True), axis=1, keepdims=True)


def solve_kernel(
    shift_ref, idle_ref, place_ref, b_ref, damp_ref, out_ref, mass_ref, x_ref, r_ref, p_ref, q_ref, ratio_ref, part_ref
):
    stride = PAIR
    piece = piece_of((COLS, EY))
    half = COLS // 2
    column = lax.broadcasted_iota(jnp.int32, (half, EY), 0)
    zero = jnp.zeros((COLS, EY), jnp.float32)

    def load(ref, start, step):
        return jnp.concatenate(
            [ref[pl.ds(start, half, stride=2 * step), :], ref[pl.ds(start + step, half, stride=2 * step), :]],
            axis=0,
        )

    def store(start, step, value):
        out_ref[pl.ds(start, half, stride=2 * step), :] = value[:half]
        out_ref[pl.ds(start + step, half, stride=2 * step), :] = value[half:]

    def x_next(v):
        return jnp.concatenate(
            [v[half:], jnp.where(column < half - 1, pltpu.roll(v[:half], half - 1, 0), 0.0)], axis=0
        )

    def x_before(v):
        return jnp.concatenate([jnp.where(column > 0, pltpu.roll(v[half:], 1, 0), 0.0), v[:half]], axis=0)

    def y_next(v):
        return pltpu.roll(v, EY - 1, 1)

    def y_before(v):
        return pltpu.roll(v, 1, 1)

    def totals():
        return [whole_sum(part_ref[mode]) for mode in range(M_DEV)]

    place = lax.rem(place_ref[0], 4)
    wrap_odd = jnp.logical_and(place == 0, column % 2 == 1)
    wrap_even = jnp.logical_and(place == 3, column % 2 == 0)

    def damp_of(n):
        even = damp_ref[pl.ds(n, half, stride=2 * PADDED), :]
        odd = damp_ref[pl.ds(n + PADDED, half, stride=2 * PADDED), :]
        even = jnp.where(wrap_even, pltpu.roll(even, 2, 0), even)
        odd = jnp.where(wrap_odd, pltpu.roll(odd, half - 2, 0), odd)
        return jnp.concatenate([even, odd], axis=0)

    def begin(mode, carry):
        shift = shift_ref[mode]
        base = mode * NODES
        norm = zero
        for n in range(NODES):
            w = np.float32(W[n // SIDE] * W[n % SIDE])
            if n < NODES - 1:
                start = first_row(n // GROUPS) + n % GROUPS
                rows = load(b_ref, start + mode * GROUPS, stride)
            else:
                rows = zero
                for s in range(N_SPAN):
                    rest = load(b_ref, first_row(s) + PAIR - 1, stride)
                    own = pltpu.roll(rest, lax.rem(s * PIECE + EY - mode * PIECE, EY), 1)
                    rows = jnp.where(piece == s, own, rows)
            damp = damp_of(n)
            rhs = w * rows
            r_ref[base + n] = rhs
            p_ref[base + n] = zero
            x_ref[base + n] = zero
            mass_ref[base + n] = w * (damp + shift)
            norm = norm + rhs * rhs
        part_ref[mode] = norm
        ratio_ref[mode] = zero
        return carry

    lax.fori_loop(0, M_DEV, begin, 0)

    def apply(mode, carry):
        base = mode * NODES
        ratio = ratio_ref[mode]
        for j in range(SIDE):
            line = []
            for i in range(SIDE):
                n = base + i * SIDE + j
                p = r_ref[n] + ratio * p_ref[n]
                p_ref[n] = p
                line.append(p)
            image = line_image(line, W[j], x_next, x_before)
            for i in range(SIDE):
                n = base + i * SIDE + j
                q_ref[n] = image[i] + mass_ref[n] * line[i]
        curve = zero
        for i in range(SIDE):
            line = [p_ref[base + i * SIDE + j] for j in range(SIDE)]
            image = line_image(line, W[i], y_next, y_before)
            for j in range(SIDE):
                n = base + i * SIDE + j
                q = q_ref[n] + image[j]
                q_ref[n] = q
                curve = curve + q * line[j]
        part_ref[mode] = curve
        return carry

    def update(mode, carry):
        base = mode * NODES
        alpha = ratio_ref[mode]
        fresh = zero
        for n in range(NODES):
            x_ref[base + n] = x_ref[base + n] + alpha * p_ref[base + n]
            r = r_ref[base + n] - alpha * q_ref[base + n]
            r_ref[base + n] = r
            fresh = fresh + r * r
        part_ref[mode] = fresh
        return carry

    def spread(values):
        for mode in range(M_DEV):
            ratio_ref[mode] = jnp.broadcast_to(values[mode], (COLS, EY))

    def iteration(step, norm):
        lax.fori_loop(0, M_DEV, apply, 0)
        curve = totals()
        spread([norm[m] / (curve[m] + idle_ref[m]) for m in range(M_DEV)])
        for mode in range(M_DEV):
            update(mode, 0)
        fresh = totals()
        spread([fresh[m] / (norm[m] + idle_ref[m]) for m in range(M_DEV)])
        return tuple(fresh)

    norm = lax.fori_loop(0, ITERS - 1, iteration, tuple(totals()))
    lax.fori_loop(0, M_DEV, apply, 0)
    curve = totals()
    spread([norm[m] / (curve[m] + idle_ref[m]) for m in range(M_DEV)])

    def solved(mode, n):
        return x_ref[mode * NODES + n] + ratio_ref[mode] * p_ref[mode * NODES + n]

    for mode in range(M_DEV):
        for n in range(NODES - 1):
            store(first_row(n // GROUPS) + n % GROUPS + mode * GROUPS, stride, solved(mode, n))
    rests = [solved(mode, NODES - 1) for mode in range(M_DEV)]
    for s in range(N_SPAN):
        own = zero
        for mode in range(M_DEV):
            own = jnp.where(piece == mode, turn(rests[mode], (mode - s) * PIECE), own)
        store(first_row(s) + PAIR - 1, stride, own)


def f32(shape):
    return jax.ShapeDtypeStruct(shape, jnp.float32)


def call(kernel, shape, scratch=(), smem=0, n_in=0):
    full = pl.BlockSpec(memory_space=pltpu.VMEM)
    scalar = pl.BlockSpec(memory_space=pltpu.SMEM)
    many = isinstance(shape, list)
    return pl.pallas_call(
        kernel,
        out_shape=[f32(s) for s in shape] if many else f32(shape),
        in_specs=[scalar] * smem + [full] * n_in,
        out_specs=[full] * len(shape) if many else full,
        scratch_shapes=[pltpu.VMEM(s, jnp.float32) for s in scratch],
        compiler_params=pltpu.CompilerParams(vmem_limit_bytes=VMEM),
    )


def body(velocity_q, advecting, damping):
    columns = ("y", "x")
    span = ("z", "core")
    everyone = ("core", "z") + columns
    up = [(i, (i + 1) % COLS) for i in range(COLS)]
    down = [(j, i) for i, j in up]
    q_nodes = jnp.transpose(velocity_q, (1, 0, 2))
    a_nodes = jnp.transpose(advecting, (0, 2, 1, 3))

    def beside(face):
        faces = SIDE * PL_DEV
        return jnp.pad(face.reshape(faces, EY), ((0, PADDED), (0, 0))) + jnp.pad(
            damping, ((faces, PADDED - NODES), (0, 0))
        )

    from_left = lax.ppermute(beside(q_nodes[NODES - SIDE :]), columns, up)
    from_right = lax.ppermute(beside(q_nodes[:SIDE]), columns, down)
    across = lax.ppermute(damping, "x", [(i, (i + 2) % 4) for i in range(4)])
    inner = call(inner_kernel, (NODES, PL_DEV, EY), n_in=2)(q_nodes, a_nodes)
    place = lax.axis_index(columns).astype(jnp.int32)[None]
    forcing, damp_row = call(
        outer_kernel, [(N_SPAN, ROWS, EY), (4 * PADDED, EY)], scratch=((PL_DEV, EY),), smem=1, n_in=6
    )(place, inner, from_left, from_right, across, damping, a_nodes)
    device = lax.axis_index(everyone)
    coef = device * M_DEV + jnp.arange(M_DEV, dtype=jnp.int32)
    wave = jnp.where(coef < WAVES, coef, coef - WAVES + 1).astype(jnp.float32)
    shifts = LAMBDA0 + (BETA * wave) ** 2
    idle = jnp.where(coef < KEPT, 0.0, 1.0).astype(jnp.float32)
    forcing, damp_row, shifts, idle = lax.optimization_barrier((forcing, damp_row, shifts, idle))
    planes = lax.all_to_all(forcing, span, split_axis=0, concat_axis=0, tiled=True)
    damp_nodes = lax.all_gather(damp_row, "y", axis=0, tiled=True)
    planes, damp_nodes = lax.optimization_barrier((planes, damp_nodes))

    forward, backward = fourier_table()
    spectra = call(forward_kernel, (N_DEV * PAIR, EY), n_in=3)(planes, *in_two(forward))
    mine = lax.all_to_all(
        spectra.reshape(N_DEV, 1, PAIR * EY), everyone, split_axis=0, concat_axis=0, tiled=True
    )

    field, part = (M_DEV * NODES, COLS, EY), (M_DEV, COLS, EY)
    solved = call(solve_kernel, (N_DEV * PAIR, EY), scratch=(field,) * 5 + (part,) * 2, smem=3, n_in=2)(
        shifts, idle, place, mine.reshape(N_DEV * PAIR, EY), damp_nodes
    )

    modes = lax.all_to_all(
        solved.reshape(N_DEV, 1, PAIR * EY), everyone, split_axis=0, concat_axis=0, tiled=True
    )
    physical = call(inverse_kernel, (N_SPAN, ROWS, EY), n_in=3)(
        modes.reshape(N_DEV * PAIR, EY), *in_two(backward)
    )
    back = lax.all_to_all(physical, span, split_axis=0, concat_axis=0, tiled=True)
    q_new = call(final_kernel, (NODES, PL_DEV, EY), n_in=1)(back)
    return jnp.transpose(q_new, (1, 0, 2))


def solution(mesh):
    columns, span = ("y", "x"), ("z", "core")
    side = math.isqrt(COLS)
    parts = Mesh(mesh.devices.reshape(side, side, N_SPAN // 2, 2), columns + span)
    placed = (P(span, None, columns), P(None, span, None, columns), P(None, columns))
    return jax.shard_map(
        body, mesh=parts, in_specs=placed, out_specs=P(span, None, columns), check_vma=False
    )
```

```python
import math

import jax
import jax.numpy as jnp
import ml_dtypes
import numpy as np
from jax import lax
from jax.experimental import pallas as pl
from jax.experimental.pallas import tpu as pltpu
from jax.sharding import Mesh, PartitionSpec as P

ORDER = 6
SIDE = 7
NODES = 49
EY = 128
COLS = 16
PLANES = 512
PL_DEV = 64
N_SPAN = 8
N_DEV = 128
WAVES = 168
KEPT = 336
M_DEV = 3
M_ALL = N_DEV * M_DEV
GROUPS = 6
PIECE = 16
ROWS = GROUPS * PL_DEV + 8
PAIR = GROUPS * M_DEV + 1
PADDED = 56
ITERS = 8

LAMBDA0 = 0.1
VISCOSITY = 0.02
PENALTY = 100.0
BETA = 0.02
VMEM = 16 * 1024 * 1024


def gll_tables(degree):
    side_nodes = degree + 1
    points = [-math.cos(math.pi * n / degree) for n in range(side_nodes)]
    values = [1.0] * side_nodes
    for _ in range(60):
        updated = []
        new_values = []
        for point in points:
            lower = 1.0
            now = point
            for step in range(2, degree + 1):
                lower, now = now, ((2 * step - 1) * point * now - (step - 1) * lower) / step
            updated.append(point - (point * now - lower) / (side_nodes * now))
            new_values.append(now)
        points = updated
        values = new_values
    weights = np.array([2.0 / (degree * side_nodes * v * v) for v in values])
    derivative = np.zeros((side_nodes, side_nodes))
    for row in range(side_nodes):
        for col in range(side_nodes):
            if row != col:
                derivative[row, col] = values[row] / (values[col] * (points[row] - points[col]))
    derivative[0, 0] = -degree * side_nodes / 4.0
    derivative[degree, degree] = degree * side_nodes / 4.0
    return weights, derivative


W, D = gll_tables(ORDER)
EDGE = 1.0 / (2.0 * W[0] * VISCOSITY)


def fourier_table():
    row = np.arange(M_ALL)[:, None]
    c = row % N_DEV * M_DEV + row // N_DEV
    p = np.arange(PLANES)[None, :]
    k = np.where(c < WAVES, c, c - WAVES + 1)
    phases = ((k * p) % PLANES) * (2.0 * math.pi / PLANES)
    table = np.where(c < WAVES, np.cos(phases), np.sin(phases))
    scale = np.where(c == 0, 1.0 / PLANES, 2.0 / PLANES)
    table = np.where(c < KEPT, table, 0.0)
    return table * scale, table.T


def in_two(table):
    table = table.astype(np.float32)
    high = table.astype(ml_dtypes.bfloat16)
    low = (table - high.astype(np.float32)).astype(ml_dtypes.bfloat16)
    return jnp.asarray(high), jnp.asarray(low)


def split(x):
    high = x.astype(jnp.bfloat16)
    low = (x - high.astype(jnp.float32)).astype(jnp.bfloat16)
    return high, low


def dot(a, b):
    return jnp.dot(a, b, preferred_element_type=jnp.float32)


def combine(coefs, values):
    total = None
    for c, v in zip(coefs, values):
        if c == 0.0:
            continue
        term = v * np.float32(c)
        total = term if total is None else total + term
    return total


def turn(x, by):
    by = by % EY
    return pltpu.roll(x, by, 1) if by else x


def piece_of(shape):
    return lax.broadcasted_iota(jnp.int32, shape, 1) // PIECE


def pack(blocks, turns):
    piece = piece_of(blocks[0].shape)
    out = turn(blocks[0], turns[0])
    for h in range(1, len(blocks)):
        out = jnp.where(piece == h, turn(blocks[h], turns[h]), out)
    return out


def inner_kernel(q_ref, a_ref, out_ref):
    table = D / VISCOSITY
    own = table.copy()
    own[6, 6] -= EDGE
    own[0, 0] += EDGE
    edge = np.float32(EDGE)

    def block(b, carry):
        rows = pl.ds(pl.multiple_of(b * 16, 16), 16)
        for i in range(SIDE):
            line = [q_ref[i * SIDE + j, rows, :] for j in range(SIDE)]
            gy = [combine(own[j], line) for j in range(SIDE)]
            gy[6] = gy[6] + edge * pltpu.roll(line[0], EY - 1, 1)
            gy[0] = gy[0] - edge * pltpu.roll(line[6], 1, 1)
            for j in range(SIDE):
                n = i * SIDE + j
                gx = combine(own[i], [q_ref[a * SIDE + j, rows, :] for a in range(SIDE)])
                ax = a_ref[0, n, rows, :].astype(jnp.float32)
                ay = a_ref[1, n, rows, :].astype(jnp.float32)
                out_ref[n, rows, :] = np.float32(LAMBDA0) * line[j] - (ax * gx + ay * gy[j])
        return carry

    lax.fori_loop(0, PL_DEV // 16, block, 0)


def outer_kernel(
    place_ref, inner_ref, left_ref, right_ref, across_ref, damp_ref, a_ref, out_ref, row_ref, last_ref
):
    column = place_ref[0]
    has_left = jnp.where(column > 0, 1.0, 0.0)
    has_right = jnp.where(column < COLS - 1, 1.0, 0.0)
    edge = np.float32(EDGE)
    for n in range(NODES):
        target = last_ref if n == NODES - 1 else out_ref.at[n // GROUPS]
        start = 0 if n == NODES - 1 else n % GROUPS * PL_DEV
        j = n % SIDE
        face = slice(j * PL_DEV, (j + 1) * PL_DEV)
        value = inner_ref[n]
        if n < SIDE:
            value = value + (edge * has_left) * left_ref[face, :] * a_ref[0, n].astype(jnp.float32)
        if n >= NODES - SIDE:
            value = value - (edge * has_right) * right_ref[face, :] * a_ref[0, n].astype(jnp.float32)
        target[start : start + PL_DEV, :] = value
    for s in range(N_SPAN):
        blocks = [last_ref[8 * h : 8 * h + 8, :] for h in range(8)]
        out_ref[s, GROUPS * PL_DEV :, :] = pack(blocks, [PIECE * (h - s) for h in range(8)])
    x = lax.rem(column, 4)
    row_ref[...] = jnp.zeros(row_ref.shape, jnp.float32)
    faces = SIDE * PL_DEV
    for step, rows in ((0, damp_ref[...]), (1, right_ref[faces:, :]), (2, across_ref[...]), (3, left_ref[faces:, :])):
        row_ref[pl.ds(pl.multiple_of(lax.rem(x + step, 4) * PADDED, 8), NODES), :] = rows[:NODES]


def product(table_refs, x):
    high, low = table_refs
    xh, xl = split(x)
    return dot(high[...], xh) + (dot(high[...], xl) + dot(low[...], xh))


def forward_kernel(x_ref, high_ref, low_ref, out_ref):
    table = (high_ref, low_ref)
    for start in range(0, GROUPS, 2):
        x = jnp.concatenate(
            [
                jnp.concatenate([x_ref[s, g * PL_DEV : (g + 1) * PL_DEV, :] for s in range(N_SPAN)], axis=0)
                for g in (start, start + 1)
            ],
            axis=1,
        )
        res = product(table, x)
        for g in range(2):
            for j in range(M_DEV):
                out_ref[pl.ds(j * GROUPS + start + g, N_DEV, stride=PAIR), :] = res[
                    j * N_DEV : (j + 1) * N_DEV, g * EY : (g + 1) * EY
                ]
    packed = [x_ref[s, GROUPS * PL_DEV :, :] for s in range(N_SPAN)]
    x = jnp.concatenate([turn(packed[s], -PIECE * h) for s in range(N_SPAN) for h in range(8)], axis=0)
    res = product(table, x)
    parts = [res[j * N_DEV : (j + 1) * N_DEV] for j in range(M_DEV)]
    out_ref[pl.ds(PAIR - 1, N_DEV, stride=PAIR), :] = pack(parts, [PIECE * j for j in range(M_DEV)])


def inverse_kernel(x_ref, high_ref, low_ref, out_ref):
    table = (high_ref, low_ref)
    for start in range(0, GROUPS, 2):
        x = jnp.concatenate(
            [
                jnp.concatenate(
                    [x_ref[pl.ds(j * GROUPS + g, N_DEV, stride=PAIR), :] for j in range(M_DEV)], axis=0
                )
                for g in (start, start + 1)
            ],
            axis=1,
        )
        res = product(table, x)
        for g in range(2):
            for s in range(N_SPAN):
                out_ref[s, (start + g) * PL_DEV : (start + g + 1) * PL_DEV, :] = res[
                    s * PL_DEV : (s + 1) * PL_DEV, g * EY : (g + 1) * EY
                ]
    rest = x_ref[pl.ds(PAIR - 1, N_DEV, stride=PAIR), :]
    x = jnp.concatenate([turn(rest, -PIECE * j) for j in range(M_DEV)], axis=0)
    res = product(table, x)
    for s in range(N_SPAN):
        blocks = [res[s * PL_DEV + 8 * h : s * PL_DEV + 8 * h + 8] for h in range(8)]
        out_ref[s, GROUPS * PL_DEV :, :] = pack(blocks, [PIECE * h for h in range(8)])


def final_kernel(x_ref, out_ref):
    for s in range(N_SPAN):
        for g in range(GROUPS):
            out_ref[s * GROUPS + g] = x_ref[s, g * PL_DEV : (g + 1) * PL_DEV, :]
    packed = [x_ref[s, GROUPS * PL_DEV :, :] for s in range(N_SPAN)]
    for h in range(8):
        out_ref[NODES - 1, 8 * h : 8 * h + 8, :] = pack(packed, [PIECE * (s - h) for s in range(N_SPAN)])


def solve_tables():
    own = D.T @ np.diag(W) @ D
    own[6, 6] += PENALTY
    own[6, :] -= D[6, :] / 2
    own[:, 6] -= D[6, :] / 2
    own[0, 0] += PENALTY
    own[0, :] += D[0, :] / 2
    own[:, 0] += D[0, :] / 2
    return own


OWN = solve_tables()


def line_image(v, weight, from_next, from_before):
    own, d6, penalty = OWN * weight, D[6] * weight, np.float32(PENALTY * weight)
    even = [v[0] + v[6], v[1] + v[5], v[2] + v[4], v[3]]
    odd = [v[0] - v[6], v[1] - v[5], v[2] - v[4]]
    d_even = [(d6[a] + d6[6 - a]) / 2 for a in range(3)] + [d6[3]]
    d_odd = [(d6[a] - d6[6 - a]) / 2 for a in range(3)]
    half_even = combine([c / 2 for c in d_even], even)
    half_odd = combine([c / 2 for c in d_odd], odd)
    first = penalty * v[0] + (half_odd - half_even)
    last = penalty * v[6] - (half_even + half_odd)
    next_value = from_next(v[0])
    next_first = from_next(first)
    before_value = from_before(v[6])
    before_last = from_before(last)
    sum_value = next_value + before_value
    dif_value = next_value - before_value
    out = [None] * SIDE
    for i in range(3):
        e = combine(
            [(own[i, a] + own[i, 6 - a]) / 2 for a in range(3)] + [own[i, 3], d_even[i] / 2],
            even + [sum_value],
        )
        o = combine(
            [(own[i, a] - own[i, 6 - a]) / 2 for a in range(3)] + [d_odd[i] / 2],
            odd + [dif_value],
        )
        out[i] = e + o
        out[6 - i] = e - o
    out[3] = combine([own[3, a] for a in range(4)] + [d6[3] / 2], even + [sum_value])
    out[6] = out[6] - next_first
    out[0] = out[0] - before_last
    return out


def first_row(s):
    return (s % 2 * (N_SPAN // 2) + s // 2) * COLS * PAIR


def whole_sum(x):
    return jnp.sum(jnp.sum(x, axis=0, keepdims=True), axis=1, keepdims=True)


def solve_kernel(
    shift_ref, idle_ref, place_ref, b_ref, damp_ref, out_ref, mass_ref, x_ref, r_ref, p_ref, q_ref, ratio_ref, part_ref
):
    stride = PAIR
    piece = piece_of((COLS, EY))
    half = COLS // 2
    column = lax.broadcasted_iota(jnp.int32, (half, EY), 0)
    zero = jnp.zeros((COLS, EY), jnp.float32)

    def load(ref, start, step):
        return jnp.concatenate(
            [ref[pl.ds(start, half, stride=2 * step), :], ref[pl.ds(start + step, half, stride=2 * step), :]],
            axis=0,
        )

    def store(start, step, value):
        out_ref[pl.ds(start, half, stride=2 * step), :] = value[:half]
        out_ref[pl.ds(start + step, half, stride=2 * step), :] = value[half:]

    def x_next(v):
        return jnp.concatenate(
            [v[half:], jnp.where(column < half - 1, pltpu.roll(v[:half], half - 1, 0), 0.0)], axis=0
        )

    def x_before(v):
        return jnp.concatenate([jnp.where(column > 0, pltpu.roll(v[half:], 1, 0), 0.0), v[:half]], axis=0)

    def y_next(v):
        return pltpu.roll(v, EY - 1, 1)

    def y_before(v):
        return pltpu.roll(v, 1, 1)

    def totals():
        return [whole_sum(part_ref[mode]) for mode in range(M_DEV)]

    place = lax.rem(place_ref[0], 4)
    wrap_odd = jnp.logical_and(place == 0, column % 2 == 1)
    wrap_even = jnp.logical_and(place == 3, column % 2 == 0)

    def damp_of(n):
        even = damp_ref[pl.ds(n, half, stride=2 * PADDED), :]
        odd = damp_ref[pl.ds(n + PADDED, half, stride=2 * PADDED), :]
        even = jnp.where(wrap_even, pltpu.roll(even, 2, 0), even)
        odd = jnp.where(wrap_odd, pltpu.roll(odd, half - 2, 0), odd)
        return jnp.concatenate([even, odd], axis=0)

    norms = [zero] * M_DEV
    rests = [load(b_ref, first_row(s) + PAIR - 1, stride) for s in range(N_SPAN)]
    for n in range(NODES):
        w = np.float32(W[n // SIDE] * W[n % SIDE])
        damp = w * damp_of(n)
        for mode in range(M_DEV):
            if n < NODES - 1:
                rows = load(b_ref, first_row(n // GROUPS) + n % GROUPS + mode * GROUPS, stride)
            else:
                rows = pack(rests, [(s - mode) * PIECE for s in range(N_SPAN)])
            rhs = w * rows
            r_ref[mode * NODES + n] = rhs
            p_ref[mode * NODES + n] = zero
            x_ref[mode * NODES + n] = zero
            mass_ref[mode * NODES + n] = damp + w * shift_ref[mode]
            norms[mode] = norms[mode] + rhs * rhs
    for mode in range(M_DEV):
        part_ref[mode] = norms[mode]
        ratio_ref[mode] = zero

    def apply(mode, carry):
        base = mode * NODES
        ratio = ratio_ref[mode]
        for j in range(SIDE):
            line = []
            for i in range(SIDE):
                n = base + i * SIDE + j
                p = r_ref[n] + ratio * p_ref[n]
                p_ref[n] = p
                line.append(p)
            image = line_image(line, W[j], x_next, x_before)
            for i in range(SIDE):
                n = base + i * SIDE + j
                q_ref[n] = image[i] + mass_ref[n] * line[i]
        curve = zero
        for i in range(SIDE):
            line = [p_ref[base + i * SIDE + j] for j in range(SIDE)]
            image = line_image(line, W[i], y_next, y_before)
            for j in range(SIDE):
                n = base + i * SIDE + j
                q = q_ref[n] + image[j]
                q_ref[n] = q
                curve = curve + q * line[j]
        part_ref[mode] = curve
        return carry

    def update(mode, carry):
        base = mode * NODES
        alpha = ratio_ref[mode]
        fresh = zero
        for n in range(NODES):
            x_ref[base + n] = x_ref[base + n] + alpha * p_ref[base + n]
            r = r_ref[base + n] - alpha * q_ref[base + n]
            r_ref[base + n] = r
            fresh = fresh + r * r
        part_ref[mode] = fresh
        return carry

    def spread(values):
        for mode in range(M_DEV):
            ratio_ref[mode] = jnp.broadcast_to(values[mode], (COLS, EY))

    def iteration(step, norm):
        lax.fori_loop(0, M_DEV, apply, 0)
        curve = totals()
        spread([norm[m] / (curve[m] + idle_ref[m]) for m in range(M_DEV)])
        for mode in range(M_DEV):
            update(mode, 0)
        fresh = totals()
        spread([fresh[m] / (norm[m] + idle_ref[m]) for m in range(M_DEV)])
        return tuple(fresh)

    norm = lax.fori_loop(0, ITERS - 1, iteration, tuple(totals()))
    lax.fori_loop(0, M_DEV, apply, 0)
    curve = totals()
    spread([norm[m] / (curve[m] + idle_ref[m]) for m in range(M_DEV)])

    def solved(mode, n):
        return x_ref[mode * NODES + n] + ratio_ref[mode] * p_ref[mode * NODES + n]

    for mode in range(M_DEV):
        for n in range(NODES - 1):
            store(first_row(n // GROUPS) + n % GROUPS + mode * GROUPS, stride, solved(mode, n))
    rests = [solved(mode, NODES - 1) for mode in range(M_DEV)]
    for s in range(N_SPAN):
        own = zero
        for mode in range(M_DEV):
            own = jnp.where(piece == mode, turn(rests[mode], (mode - s) * PIECE), own)
        store(first_row(s) + PAIR - 1, stride, own)


def f32(shape):
    return jax.ShapeDtypeStruct(shape, jnp.float32)


def call(kernel, shape, scratch=(), smem=0, n_in=0):
    full = pl.BlockSpec(memory_space=pltpu.VMEM)
    scalar = pl.BlockSpec(memory_space=pltpu.SMEM)
    many = isinstance(shape, list)
    return pl.pallas_call(
        kernel,
        out_shape=[f32(s) for s in shape] if many else f32(shape),
        in_specs=[scalar] * smem + [full] * n_in,
        out_specs=[full] * len(shape) if many else full,
        scratch_shapes=[pltpu.VMEM(s, jnp.float32) for s in scratch],
        compiler_params=pltpu.CompilerParams(vmem_limit_bytes=VMEM),
    )


def body(velocity_q, advecting, damping):
    columns = ("y", "x")
    span = ("z", "core")
    everyone = ("core", "z") + columns
    up = [(i, (i + 1) % COLS) for i in range(COLS)]
    down = [(j, i) for i, j in up]
    q_nodes = jnp.transpose(velocity_q, (1, 0, 2))
    a_nodes = jnp.transpose(advecting, (0, 2, 1, 3))

    def beside(face):
        faces = SIDE * PL_DEV
        return jnp.pad(face.reshape(faces, EY), ((0, PADDED), (0, 0))) + jnp.pad(
            damping, ((faces, PADDED - NODES), (0, 0))
        )

    from_left = lax.ppermute(beside(q_nodes[NODES - SIDE :]), columns, up)
    from_right = lax.ppermute(beside(q_nodes[:SIDE]), columns, down)
    across = lax.ppermute(damping, "x", [(i, (i + 2) % 4) for i in range(4)])
    inner = call(inner_kernel, (NODES, PL_DEV, EY), n_in=2)(q_nodes, a_nodes)
    place = lax.axis_index(columns).astype(jnp.int32)[None]
    forcing, damp_row = call(
        outer_kernel, [(N_SPAN, ROWS, EY), (4 * PADDED, EY)], scratch=((PL_DEV, EY),), smem=1, n_in=6
    )(place, inner, from_left, from_right, across, damping, a_nodes)
    device = lax.axis_index(everyone)
    coef = device * M_DEV + jnp.arange(M_DEV, dtype=jnp.int32)
    wave = jnp.where(coef < WAVES, coef, coef - WAVES + 1).astype(jnp.float32)
    shifts = LAMBDA0 + (BETA * wave) ** 2
    idle = jnp.where(coef < KEPT, 0.0, 1.0).astype(jnp.float32)
    forcing, damp_row, shifts, idle = lax.optimization_barrier((forcing, damp_row, shifts, idle))
    planes = lax.all_to_all(forcing, span, split_axis=0, concat_axis=0, tiled=True)
    damp_nodes = lax.all_gather(damp_row, "y", axis=0, tiled=True)
    planes, damp_nodes = lax.optimization_barrier((planes, damp_nodes))

    forward, backward = fourier_table()
    spectra = call(forward_kernel, (N_DEV * PAIR, EY), n_in=3)(planes, *in_two(forward))
    mine = lax.all_to_all(
        spectra.reshape(N_DEV, 1, PAIR * EY), everyone, split_axis=0, concat_axis=0, tiled=True
    )

    field, part = (M_DEV * NODES, COLS, EY), (M_DEV, COLS, EY)
    solved = call(solve_kernel, (N_DEV * PAIR, EY), scratch=(field,) * 5 + (part,) * 2, smem=3, n_in=2)(
        shifts, idle, place, mine.reshape(N_DEV * PAIR, EY), damp_nodes
    )

    modes = lax.all_to_all(
        solved.reshape(N_DEV, 1, PAIR * EY), everyone, split_axis=0, concat_axis=0, tiled=True
    )
    physical = call(inverse_kernel, (N_SPAN, ROWS, EY), n_in=3)(
        modes.reshape(N_DEV * PAIR, EY), *in_two(backward)
    )
    back = lax.all_to_all(physical, span, split_axis=0, concat_axis=0, tiled=True)
    q_new = call(final_kernel, (NODES, PL_DEV, EY), n_in=1)(back)
    return jnp.transpose(q_new, (1, 0, 2))


def solution(mesh):
    columns, span = ("y", "x"), ("z", "core")
    side = math.isqrt(COLS)
    parts = Mesh(mesh.devices.reshape(side, side, N_SPAN // 2, 2), columns + span)
    placed = (P(span, None, columns), P(None, span, None, columns), P(None, columns))
    return jax.shard_map(
        body, mesh=parts, in_specs=placed, out_specs=P(span, None, columns), check_vma=False
    )
```
